32 devices in a mesh: dp: 8 (over z, y), fsdp: 4 (over x, core).
Axes of the slice: x: 2, y: 2, z: 4, core: 2. Of those that a mesh axis runs over, the one named last changes fastest.
Arguments:
- images: bfloat16 [32, 32, 128, 256], P(('dp', 'fsdp')), may hold values from -6 to 6
- targets: bfloat16 [32, 32, 128, 256], P(('dp', 'fsdp')), may hold values from -6 to 6
- pixel_mask: int32 [32, 32, 128], P(('dp', 'fsdp')), may hold values from 0 to 1, as said below
- encfirst: bfloat16 [2304, 64], P('dp', 'fsdp'), may hold values from -0.125 to 0.125
- encsecond: bfloat16 [576, 64], P('dp', 'fsdp'), may hold values from -0.25 to 0.25
- encthird: bfloat16 [576, 64], P('dp', 'fsdp'), may hold values from -0.25 to 0.25
- encfourth: bfloat16 [64, 256], P('dp', 'fsdp'), may hold values from -96 to 96
- encbiasa: bfloat16 [64], P('dp'), may hold values from -1 to 1
- encbiasb: bfloat16 [64], P('dp'), may hold values from -1 to 1
- encbiasc: bfloat16 [64], P('dp'), may hold values from -1 to 1
- encbiasd: bfloat16 [256], P('dp'), may hold values from -1 to 1
- decfirst: bfloat16 [256, 64], P('dp', 'fsdp'), may hold values from -0.375 to 0.375
- decsecond: bfloat16 [576, 64], P('dp', 'fsdp'), may hold values from -0.25 to 0.25
- decthird: bfloat16 [576, 64], P('dp', 'fsdp'), may hold values from -0.25 to 0.25
- decfourth: bfloat16 [576, 256], P('dp', 'fsdp'), may hold values from -24 to 24
- decbiasa: bfloat16 [64], P('dp'), may hold values from -1 to 1
- decbiasb: bfloat16 [64], P('dp'), may hold values from -1 to 1
- decbiasc: bfloat16 [64], P('dp'), may hold values from -1 to 1
- decbiasd: bfloat16 [256], P('dp'), may hold values from -1 to 1
Outputs:
- decoded: bfloat16 [32, 32, 128, 256], P(('dp', 'fsdp'))
- images_grad: bfloat16 [32, 32, 128, 256], P(('dp', 'fsdp'))
- image_loss: float32 [32], P(('dp', 'fsdp'))
- encfirst_grad: float32 [2304, 64], P('dp', 'fsdp')
- encsecond_grad: float32 [576, 64], P('dp', 'fsdp')
- encthird_grad: float32 [576, 64], P('dp', 'fsdp')
- encfourth_grad: float32 [64, 256], P('dp', 'fsdp')
- encbiasa_grad: float32 [64], P('dp')
- encbiasb_grad: float32 [64], P('dp')
- encbiasc_grad: float32 [64], P('dp')
- encbiasd_grad: float32 [256], P('dp')
- decfirst_grad: float32 [256, 64], P('dp', 'fsdp')
- decsecond_grad: float32 [576, 64], P('dp', 'fsdp')
- decthird_grad: float32 [576, 64], P('dp', 'fsdp')
- decfourth_grad: float32 [576, 256], P('dp', 'fsdp')
- decbiasa_grad: float32 [64], P('dp')
- decbiasb_grad: float32 [64], P('dp')
- decbiasc_grad: float32 [64], P('dp')
- decbiasd_grad: float32 [256], P('dp')
The draws below stay inside these ranges and needn't reach their ends.
Inputs may be any that keep to these rules, and one draw needn't show every extreme that they name: `pixel_mask`: each image's mask is 1 on the rectangle of its first rows and first columns, at least 16 rows and 64 columns, and 0 elsewhere; at least its last row and its last column are 0.
All inputs are finite; a program needn't handle non-finite values.
Results may differ from the reference program's by a relative error of at most 0.0066.
Values may be sent and summed in bfloat16 or wider, within the bound.
A program may use at most 128 MiB of HBM per device.

```python
import jax
import jax.numpy as jnp
from jax import lax

CH = 256
HC = 64
IMG_H = 32
IMG_W = 128
IMAGES = 32


def draw_pixel_mask(key, part):
    key = jax.random.fold_in(key, 7)
    row_key, col_key = jax.random.split(key)
    heights = jax.random.randint(row_key, (IMAGES, 1, 1), IMG_H // 2, IMG_H, dtype=jnp.int32)
    widths = jax.random.randint(col_key, (IMAGES, 1, 1), IMG_W // 2, IMG_W, dtype=jnp.int32)
    row_index = jnp.arange(IMG_H, dtype=jnp.int32).reshape(1, IMG_H, 1)
    col_index = jnp.arange(IMG_W, dtype=jnp.int32).reshape(1, 1, IMG_W)
    return ((row_index < heights) & (col_index < widths)).astype(jnp.int32)


def level_of(key, dims, cuts, smallest, largest):
    level = 1.0
    for position, blocks in cuts:
        draws = jax.random.uniform(jax.random.fold_in(jax.random.fold_in(key, 6), position), (blocks,), jnp.float32, smallest / len(cuts), largest / len(cuts))
        level = level * jnp.repeat(jnp.exp(draws), dims[position] // blocks).reshape((-1,) + (1,) * (len(dims) - 1 - position))
    return level


def centred(key, dims, width, bound, cuts=(), kind=jnp.bfloat16):
    array = jax.random.normal(key, dims, jnp.float32) * width
    if len(cuts) > 0:
        array = level_of(key, dims, cuts, -0.22, 0.18) * array
    return jnp.clip(array, min=-bound, max=bound).astype(kind)


def setup_inputs(seed: int = 0) -> dict:
    key_list = jax.random.split(jax.random.key(seed), 20)
    return {
        "images": centred(key_list[0], (IMAGES, IMG_H, IMG_W, CH), 1.0, 6.0, ((0, 32),)),
        "targets": centred(key_list[1], (IMAGES, IMG_H, IMG_W, CH), 1.0, 6.0, ((0, 32),)),
        "pixel_mask": draw_pixel_mask(jax.random.fold_in(key_list[19], 71), 0),
        "encfirst": centred(key_list[3], (9 * CH, HC), (9 * CH) ** -0.5, 0.125, ((0, 8), (1, 4))),
        "encsecond": centred(key_list[4], (9 * HC, HC), (9 * HC) ** -0.5, 0.25, ((0, 8), (1, 4))),
        "encthird": centred(key_list[5], (9 * HC, HC), (9 * HC) ** -0.5, 0.25, ((0, 8), (1, 4))),
        "encfourth": centred(key_list[6], (HC, CH), 16.0, 96.0, ((0, 8), (1, 4))),
        "encbiasa": centred(key_list[7], (HC,), 0.2, 1.0, ((0, 8),)),
        "encbiasb": centred(key_list[8], (HC,), 0.2, 1.0, ((0, 8),)),
        "encbiasc": centred(key_list[9], (HC,), 0.2, 1.0, ((0, 8),)),
        "encbiasd": centred(key_list[10], (CH,), 0.2, 1.0, ((0, 8),)),
        "decfirst": centred(key_list[11], (CH, HC), CH ** -0.5, 0.375, ((0, 8), (1, 4))),
        "decsecond": centred(key_list[12], (9 * HC, HC), (9 * HC) ** -0.5, 0.25, ((0, 8), (1, 4))),
        "decthird": centred(key_list[13], (9 * HC, HC), (9 * HC) ** -0.5, 0.25, ((0, 8), (1, 4))),
        "decfourth": centred(key_list[14], (9 * HC, CH), 4.0, 24.0, ((0, 8), (1, 4))),
        "decbiasa": centred(key_list[15], (HC,), 0.2, 1.0, ((0, 8),)),
        "decbiasb": centred(key_list[16], (HC,), 0.2, 1.0, ((0, 8),)),
        "decbiasc": centred(key_list[17], (HC,), 0.2, 1.0, ((0, 8),)),
        "decbiasd": centred(key_list[18], (CH,), 0.2, 1.0, ((0, 8),)),
    }


@jax.custom_vjp
def low(v):
    return lax.optimization_barrier(v.astype(jnp.bfloat16)).astype(jnp.float32)

@jax.custom_vjp
def low_back(v):
    return v

def low_keep(v):
    return (low(v), None)

def low_pass(kept, grad):
    return (grad,)

def back_keep(v):
    return (v, None)

def back_low(kept, grad):
    return (low(grad),)
low.defvjp(low_keep, low_pass)
low_back.defvjp(back_keep, back_low)
post_gain = 1.0 / 64.0

def conv_any(inputs, kernel):
    channels = inputs.shape[-1]
    if kernel.shape[0] == channels:
        return jnp.dot(inputs, kernel, precision=lax.Precision.HIGHEST)
    kernel_taps = kernel.reshape(3, 3, channels, kernel.shape[1])
    output = lax.conv_general_dilated(inputs[None], kernel_taps, (1, 1), ((1, 1), (1, 1)), dimension_numbers=('NHWC', 'HWIO', 'NHWC'), precision=lax.Precision.HIGHEST)
    return output[0]

def branch(first_act, kernels, offsets):
    current = first_act
    for layer_num in range(3):
        current = low(jax.nn.silu(low_back(conv_any(current, kernels[layer_num]) + offsets[layer_num])))
    return low_back(conv_any(current, kernels[3]) + offsets[3])

def forward(params, source, goal_image, weights_mask):
    middle = source + branch(low(jax.nn.silu(source)), params[0:4], params[4:8]) * post_gain
    result = middle + branch(low(jax.nn.silu(middle)), params[8:12], params[12:16]) * post_gain
    residual = result - goal_image
    return (0.5 * jnp.sum(weights_mask * residual * residual), result)

def reference(images, targets, pixel_mask, encfirst, encsecond, encthird, encfourth, encbiasa, encbiasb, encbiasc, encbiasd, decfirst, decsecond, decthird, decfourth, decbiasa, decbiasb, decbiasc, decbiasd):
    params = tuple((weight.astype(jnp.float32) for weight in (encfirst, encsecond, encthird, encfourth, encbiasa, encbiasb, encbiasc, encbiasd, decfirst, decsecond, decthird, decfourth, decbiasa, decbiasb, decbiasc, decbiasd)))

    def one_image(totals, inputs):
        picture, target, mask_img = inputs
        source = picture.astype(jnp.float32)
        goal_image = target.astype(jnp.float32)
        weights_mask = mask_img.astype(jnp.float32)[:, :, None]

        def objective(weights, entry_image):
            return forward(weights, entry_image, goal_image, weights_mask)
        err_total, pullback, result = jax.vjp(objective, params, source, has_aux=True)
        weight_grads, source_grad = pullback(jnp.ones_like(err_total))
        totals = jax.tree.map(jnp.add, totals, weight_grads)
        image_loss = err_total / (jnp.sum(weights_mask) * result.shape[-1])
        return (totals, (result.astype(jnp.bfloat16), source_grad.astype(jnp.bfloat16), image_loss))
    initial = tuple((jnp.zeros_like(weight) for weight in params))
    totals, stacked = lax.scan(one_image, initial, (images, targets, pixel_mask))
    return (stacked[0], stacked[1], stacked[2], totals[0], totals[1], totals[2], totals[3], totals[4], totals[5], totals[6], totals[7], totals[8], totals[9], totals[10], totals[11], totals[12], totals[13], totals[14], totals[15])
```

```python
import functools
import jax
import jax.numpy as jnp
from jax import lax
from jax.experimental import pallas as pl
from jax.experimental.pallas import tpu as pltpu
from jax.sharding import PartitionSpec as P

F32, BF16 = jnp.float32, jnp.bfloat16


def dot(a, b):
    return jnp.dot(a, b, preferred_element_type=F32)


def dot_t(a, b):
    return lax.dot_general(a, b, (((1,), (1,)), ((), ())), preferred_element_type=F32)


def dot_p(a, b):
    return lax.dot_general(a, b, (((0,), (0,)), ((), ())), preferred_element_type=F32)


def loop(count, body, unroll):
    if unroll >= count:
        for c in range(count):
            body(c)
    else:
        def step(k, _):
            for u in range(unroll):
                body(k * unroll + u)
            return 0
        lax.fori_loop(0, count // unroll, step, 0)


def masks():
    lane = lax.broadcasted_iota(jnp.int32, (1, 1, 8, 128), 3)
    row = lax.broadcasted_iota(jnp.int32, (1, 1, 8, 128), 2)
    return lane < 64, row


def shifted(x):
    n = x.shape[0]
    _, row = masks()
    x4 = x.reshape(n, 8, 8, 128)
    nxt = jnp.where(row == 7, 0.0, pltpu.roll(x4[:, :1], 7, 2))
    prv = jnp.where(row == 0, 0.0, pltpu.roll(x4[:, 7:], 1, 2))
    up = jnp.concatenate([x4[:, 1:], nxt], axis=1)
    dn = jnp.concatenate([prv, x4[:, :7]], axis=1)
    return up, dn


def beside(x):
    lo, _ = masks()
    up, dn = shifted(x)
    return jnp.where(lo, up, dn).reshape(x.shape)


def folded(x):
    lo, _ = masks()
    up, dn = shifted(x)
    return jnp.where(lo, dn, up).reshape(x.shape)


def silu_parts(v):
    h = 0.5 * v
    u = 1.0 + jnp.tanh(h)
    act = h * u
    w = 0.5 * u
    return act, w + act * (1.0 - w)


def part_sum(x):
    return x.reshape(-1, 8, x.shape[-1]).sum(axis=0)


def put_pair(ref, idx, x):
    n = x.shape[0]
    ref[pl.ds(idx, n), :, 0:128] = x.astype(BF16)
    ref[pl.ds(idx, n), :, 128:256] = beside(x).astype(BF16)


def quad_rows(ref, r0, n, d):
    return jnp.concatenate([ref[2 * (r0 + k) + d] for k in range(n)], axis=0)


def split_rows(acc, n):
    a = acc.reshape(n, 1, 64, 256)
    return jnp.concatenate([a[..., :128], a[..., 128:]], axis=1).reshape(2 * n, 64, 128)


def taps(k, i, rows):
    return [k[(3 * i + j) * rows:(3 * i + j + 1) * rows] for j in range(3)]


def spread_in(k, i, rows):
    k0, k1, k2 = taps(k, i, rows)
    z = jnp.zeros_like(k0)
    top = jnp.concatenate([k1, k0, z, k2], axis=1)
    bot = jnp.concatenate([k2, k1, k0, z], axis=1)
    return jnp.concatenate([top, bot], axis=0)


def spread_out(k, i, rows):
    k0, k1, k2 = taps(k, i, rows)
    z = jnp.zeros_like(k0)
    return jnp.concatenate([
        jnp.concatenate([k1, k0], axis=1),
        jnp.concatenate([k2, k1], axis=1),
        jnp.concatenate([z, k2], axis=1),
        jnp.concatenate([k0, z], axis=1)], axis=0)


def compute_kernel(U, *refs):
    (images, targets, mask, ef, es, et, eo, df, ds_, dt, do, eba, ebb, ebc, ebd, dba, dbb, dbc, dbd,
     decoded, images_grad, loss,
     g_ef, g_es, g_et, g_eo, g_df, g_ds, g_dt, g_do,
     gb_ea, gb_eb, gb_ec, gb_ed, gb_da, gb_db, gb_dc, gb_dd,
     src, act0, sl_src, z1, z2, a3, y1, y2, y3, s1, s2, s3, t1, t2, t3,
     mid, sl_mid, d0, g4, h4, zg, zh, stage,
     w_ef, w_es, w_et, v_es, v_et, w_ds, w_dt, v_ds, v_dt, w_do, w_eo, w_df, bias, bacc, eacc) = refs

    for ref in (act0, g4, z1, z2, y1, y2, y3, zg, zh):
        ref[0] = jnp.zeros(ref.shape[1:], ref.dtype)
        ref[33] = jnp.zeros(ref.shape[1:], ref.dtype)
    bacc[...] = jnp.zeros_like(bacc)
    eacc[...] = jnp.zeros_like(eacc)

    k = ef[...]
    for i in range(3):
        w_ef[i] = spread_in(k, i, 256)
    for k_ref, w_ref, v_ref in ((es, w_es, v_es), (et, w_et, v_et), (ds_, w_ds, v_ds), (dt, w_dt, v_dt)):
        k = k_ref[...]
        w_ref[...] = jnp.zeros_like(w_ref)
        v_ref[...] = jnp.zeros_like(v_ref)
        for i in range(3):
            f = spread_out(k, i, 64)
            w_ref[i, :, 0:128] = f
            w_ref[i + 1, :, 128:256] = f
            b = spread_in(k, i, 64)
            v_ref[2 - i, 0:128, :] = b
            v_ref[3 - i, 128:256, :] = b
    k = do[...]
    for i in range(3):
        w_do[i] = spread_out(k, i, 64)
    k = eo[...]
    z = jnp.zeros_like(k)
    w_eo[...] = jnp.concatenate([jnp.concatenate([k, z], axis=1), jnp.concatenate([z, k], axis=1)], axis=0)
    k = df[...]
    z = jnp.zeros_like(k)
    w_df[...] = jnp.concatenate([jnp.concatenate([k, z], axis=1), jnp.concatenate([z, k], axis=1)], axis=0)
    for n, b_ref in enumerate((eba, ebb, ebc, dba, dbb, dbc)):
        b = b_ref[...].astype(F32)
        bias[n, :, 0:128] = jnp.concatenate([b, b], axis=1)
    for n, b_ref in ((6, ebd), (7, dbd)):
        b = b_ref[...].astype(F32) * (1.0 / 64.0)
        bias[n] = jnp.concatenate([b, b], axis=1)

    def to_pairs(v, slot):
        stage[slot, 0] = v[:, :128]
        stage[slot, 1] = v[:, 128:]
        return [jnp.concatenate([stage[slot, h, pl.ds(2 * t + e, 8, stride=16), :] for t in range(8)], axis=0)
                for e in range(2) for h in range(2)]

    def to_natural(v, slot):
        for e in range(2):
            for h in range(2):
                for t in range(8):
                    stage[slot, h, pl.ds(2 * t + e, 8, stride=16), :] = v[8 * t:8 * t + 8, e * 256 + h * 128:e * 256 + h * 128 + 128]
        return stage[slot, 0], stage[slot, 1]

    def body(p):
        v = images[p].astype(F32)
        slot = p % 4 if isinstance(p, int) else lax.rem(p, 4)
        parts = to_pairs(v, slot)
        for q, x in enumerate(parts):
            ln = slice(q * 128, q * 128 + 128)
            act, slope = silu_parts(x)
            src[p, :, ln] = x.astype(BF16)
            act0[p + 1, :, ln] = act.astype(BF16)
            sl_src[p, :, ln] = slope
    loop(32, body, U['B'])

    def hidden(pre, b, slope_ref, row):
        act, slope = silu_parts(pre + bias[b, :, 0:128])
        slope_ref[pl.ds(row, pre.shape[0])] = slope
        return act

    n = U['nC']
    def body(c):
        p = c * n
        acc = 0.0
        for i in range(3):
            acc = acc + dot(act0[pl.ds(p + i, n)].reshape(n * 64, 512), w_ef[i])
        acc = acc.reshape(n, 64, 256)
        pre = acc[..., :128] + folded(acc[..., 128:])
        put_pair(z1, p + 1, hidden(pre, 0, s1, p))
    loop(32 // n, body, U['C'])

    def quad_conv(zin, w, b, slope_ref, zout, n, unroll, pair=True):
        def body(c):
            acc = 0.0
            for d in range(4):
                acc = acc + dot(quad_rows(zin, c * n, n, d), w[d])
            act = hidden(split_rows(acc, n), b, slope_ref, c * 2 * n)
            if pair:
                put_pair(zout, c * 2 * n + 1, act)
            else:
                zout[pl.ds(c * 2 * n, 2 * n)] = act.astype(BF16)
        loop(16 // n, body, unroll)

    quad_conv(z1, w_es, 1, s2, z2, U['nQ'], U['Q'])
    quad_conv(z2, w_et, 2, s3, a3, U['nQ'], U['Q'], pair=False)

    n = U['nF']
    def body(c):
        p = c * n
        br = dot(a3[pl.ds(p, n)].reshape(n * 64, 128), w_eo[...])
        m = src[pl.ds(p, n)].astype(F32).reshape(n * 64, 512) + (br * (1.0 / 64.0) + bias[6])
        act, slope = silu_parts(m)
        mid[pl.ds(p, n)] = m.reshape(n, 64, 512)
        sl_mid[pl.ds(p, n)] = slope.reshape(n, 64, 512)
        act = act.astype(BF16)
        d0[pl.ds(p, n)] = act.reshape(n, 64, 512)
        pre = dot(act, w_df[...]).reshape(n, 64, 128)
        put_pair(y1, p + 1, hidden(pre, 3, t1, p))
    loop(32 // n, body, U['F'])

    quad_conv(y1, w_ds, 4, t2, y2, U['nQ'], U['Q'])
    quad_conv(y2, w_dt, 5, t3, y3, U['nQ'], U['Q'])

    mk = mask[...].astype(F32)
    height = jnp.sum(mk[:, 0:1])
    width = jnp.sum(mk[0:1, :])
    sub = lax.broadcasted_iota(jnp.int32, (64, 128), 0)
    column = lax.rem(sub, 8) * 16 + 2 * (sub // 8)
    wi = width.astype(jnp.int32)
    hi = height.astype(jnp.int32)
    col_mask = [jnp.where(column + e < wi, 1.0, 0.0) for e in range(2)]
    n = U['nJ']
    def body(c):
        p = c * n
        acc = 0.0
        for i in range(3):
            acc = acc + dot(y3[pl.ds(p + i, n)].reshape(n * 64, 256), w_do[i])
        acc = acc.reshape(n, 64, 512)
        for r in range(n):
            m = mid[p + r]
            res = m + (acc[r] * (1.0 / 64.0) + bias[7])
            slot = r % 2
            a, b = to_natural(res, 2 + slot)
            decoded[p + r, :, 0:128] = a.astype(BF16)
            decoded[p + r, :, 128:256] = b.astype(BF16)
            t = to_pairs(targets[p + r].astype(F32), slot)
            row_on = jnp.where(p + r < hi, 1.0, 0.0)
            for q in range(4):
                ln = slice(q * 128, q * 128 + 128)
                diff = res[:, ln] - t[q]
                g = diff * (col_mask[q // 2] * row_on)
                mid[p + r, :, ln] = g
                eacc[...] += part_sum(g * diff)
                g = g * (1.0 / 64.0)
                g4[p + r + 1, :, ln] = g.astype(BF16)
                bacc[7, :, ln] += part_sum(g)
    loop(32 // n, body, U['J'])
    loss[0] = 0.5 * jnp.sum(eacc[...]) / (height * width * 256.0)

    def back(x, slope_ref, row, b):
        g = x * slope_ref[pl.ds(row, x.shape[0])]
        bacc[b, :, 0:128] += part_sum(g)
        return g

    n = U['nC']
    def body(c):
        p = c * n
        acc = 0.0
        for i in range(3):
            acc = acc + dot_t(g4[pl.ds(p + i, n)].reshape(n * 64, 512), w_do[2 - i])
        acc = acc.reshape(n, 64, 256)
        x = acc[..., :128] + folded(acc[..., 128:])
        put_pair(zg, p + 1, back(x, t3, p, 5))
    loop(32 // n, body, U['K'])

    def wide_wgrad(z, lo, g, n_rows=32):
        return dot_p(z[pl.ds(lo, n_rows)].reshape(n_rows * 64, z.shape[2]), g)

    M = [3, 0, 1, 2]

    gv = g4[pl.ds(1, 32)].reshape(2048, 512)
    for i in range(3):
        t = wide_wgrad(y3, i, gv)
        for j in range(3):
            a, b = M[j] * 64, M[j + 1] * 64
            g_do[(3 * i + j) * 64:(3 * i + j + 1) * 64] = t[a:a + 64, 0:256] + t[b:b + 64, 256:512]

    def quad_wgrad(z, g_ref, out):
        gq = jnp.concatenate([
            jnp.concatenate([g_ref[2 * r + 1, :, 0:128] for r in range(16)], axis=0),
            jnp.concatenate([g_ref[2 * r + 2, :, 0:128] for r in range(16)], axis=0)], axis=1)
        t = [dot_p(quad_rows(z, 0, 16, d), gq) for d in range(4)]
        for i in range(3):
            s = t[i][:, 0:128] + t[i + 1][:, 128:256]
            for j in range(3):
                a, b = M[j] * 64, M[j + 1] * 64
                v = s[a:a + 64] + pltpu.roll(s[b:b + 64], 64, 1)
                out[(3 * i + j) * 64:(3 * i + j + 1) * 64] = v[:, 0:64]

    def quad_back(zin, v, slope_ref, b, zout, n, unroll):
        def body(c):
            acc = 0.0
            for d in range(4):
                acc = acc + dot_t(quad_rows(zin, c * n, n, d), v[d])
            put_pair(zout, c * 2 * n + 1, back(split_rows(acc, n), slope_ref, c * 2 * n, b))
        loop(16 // n, body, unroll)

    quad_back(zg, v_dt, t2, 4, zh, U['nQ'], U['Q'])
    quad_wgrad(y2, zg, g_dt)
    quad_back(zh, v_ds, t1, 3, zg, U['nQ'], U['Q'])
    quad_wgrad(y1, zh, g_ds)

    t = dot_p(d0[...].reshape(2048, 512), zg[pl.ds(1, 32), :, 0:128].reshape(2048, 128))
    v = t[0:256] + pltpu.roll(t[256:512], 64, 1)
    g_df[...] = v[:, 0:64]

    n = U['nF']
    def body(c):
        p = c * n
        bk = dot_t(zg[pl.ds(p + 1, n), :, 0:128].reshape(n * 64, 128), w_df[...])
        gm = mid[pl.ds(p, n)].reshape(n * 64, 512) + sl_mid[pl.ds(p, n)].reshape(n * 64, 512) * bk
        mid[pl.ds(p, n)] = gm.reshape(n, 64, 512)
        g = gm * (1.0 / 64.0)
        bacc[6] += part_sum(g)
        g = g.astype(BF16)
        h4[pl.ds(p, n)] = g.reshape(n, 64, 512)
        x = dot_t(g, w_eo[...]).reshape(n, 64, 128)
        put_pair(zh, p + 1, back(x, s3, p, 2))
    loop(32 // n, body, U['F'])

    t = dot_p(a3[...].reshape(2048, 128), h4[...].reshape(2048, 512))
    g_eo[...] = t[0:64, 0:256] + t[64:128, 256:512]

    quad_back(zh, v_et, s2, 1, zg, U['nQ'], U['Q'])
    quad_wgrad(z2, zh, g_et)
    quad_back(zg, v_es, s1, 0, zh, U['nQ'], U['Q'])
    quad_wgrad(z1, zg, g_es)

    gv = zh[pl.ds(1, 32)].reshape(2048, 256)
    for i in range(3):
        t = wide_wgrad(act0, i, gv)
        a, b = t[0:256], t[256:512]
        outs = (
            pltpu.roll(a[:, 0:128], 64, 1) + b[:, 128:256],
            a[:, 0:128] + pltpu.roll(b[:, 0:128], 64, 1),
            pltpu.roll(a[:, 128:256], 64, 1) + b[:, 0:128])
        for j in range(3):
            g_ef[(3 * i + j) * 256:(3 * i + j + 1) * 256] = outs[j][:, 0:64]

    n = U['nJ']
    def body(c):
        p = c * n
        acc = 0.0
        for i in range(3):
            acc = acc + dot_t(zh[pl.ds(p + i, n)].reshape(n * 64, 256), w_ef[2 - i])
        acc = acc.reshape(n, 64, 512)
        for r in range(n):
            g = mid[p + r] + sl_src[p + r] * acc[r]
            a, b = to_natural(g, r % 4)
            images_grad[p + r, :, 0:128] = a.astype(BF16)
            images_grad[p + r, :, 128:256] = b.astype(BF16)
    loop(32 // n, body, U['J'])

    for n, o in enumerate((gb_ea, gb_eb, gb_ec, gb_da, gb_db, gb_dc)):
        v = jnp.sum(bacc[n, :, 0:128], axis=0, keepdims=True)
        o[...] = (v + pltpu.roll(v, 64, 1))[:, 0:64]
    for n, o in ((6, gb_ed), (7, gb_dd)):
        v = jnp.sum(bacc[n], axis=0, keepdims=True)
        o[...] = v[:, 0:256] + v[:, 256:512]


def compute(U, images, targets, mask, *weights):
    V = lambda shape, dt: pltpu.VMEM(shape, dt)
    out_shape = (
        [jax.ShapeDtypeStruct((32, 128, 256), BF16)] * 2 + [jax.ShapeDtypeStruct((1,), F32)]
        + [jax.ShapeDtypeStruct(s, F32) for s in ((2304, 64), (576, 64), (576, 64), (64, 256), (256, 64), (576, 64), (576, 64), (576, 256))]
        + [jax.ShapeDtypeStruct((1, s), F32) for s in (64, 64, 64, 256, 64, 64, 64, 256)])
    vm = pl.BlockSpec(memory_space=pltpu.VMEM)
    out_specs = [vm, vm, pl.BlockSpec(memory_space=pltpu.SMEM)] + [vm] * 16
    scratch = [
        V((32, 64, 512), BF16), V((34, 64, 512), BF16), V((32, 64, 512), F32),
        V((34, 64, 256), BF16), V((34, 64, 256), BF16), V((32, 64, 128), BF16),
        V((34, 64, 256), BF16), V((34, 64, 256), BF16), V((34, 64, 256), BF16),
        V((32, 64, 128), F32), V((32, 64, 128), F32), V((32, 64, 128), F32),
        V((32, 64, 128), F32), V((32, 64, 128), F32), V((32, 64, 128), F32),
        V((32, 64, 512), F32), V((32, 64, 512), F32), V((32, 64, 512), BF16),
        V((34, 64, 512), BF16), V((32, 64, 512), BF16), V((34, 64, 256), BF16), V((34, 64, 256), BF16),
        V((4, 2, 128, 128), F32),
        V((3, 512, 256), BF16)] + [V((4, 256, 256), BF16)] * 8 + [
        V((3, 256, 512), BF16), V((128, 512), BF16), V((512, 128), BF16),
        V((8, 1, 512), F32), V((8, 8, 512), F32), V((8, 128), F32)]
    return pl.pallas_call(
        functools.partial(compute_kernel, U), out_shape=out_shape, in_specs=[vm] * 19, out_specs=out_specs,
        scratch_shapes=scratch,
        compiler_params=pltpu.CompilerParams(vmem_limit_bytes=60 * 2**20),
    )(images, targets, mask, *weights)


U = dict(B=4, nC=8, C=1, K=1, nQ=8, Q=1, nF=4, F=1, nJ=4, J=1)


def per_device(images, targets, pixel_mask, *shards):
    order = (0, 1, 2, 3, 8, 9, 10, 11, 4, 5, 6, 7, 12, 13, 14, 15)
    shards = [shards[k] for k in order]
    dp, fs = lax.axis_size("dp"), lax.axis_size("fsdp")
    flat = jnp.concatenate([w.reshape(-1) for w in shards])
    every = lax.all_gather(flat, ("dp", "fsdp")).reshape(dp, fs, -1)
    whole, at = [], 0
    for w in shards:
        part = every[:, :, at:at + w.size]
        at += w.size
        if w.ndim == 2:
            part = part.reshape(dp, fs, *w.shape).transpose(0, 2, 1, 3).reshape(dp * w.shape[0], fs * w.shape[1])
        else:
            part = part[:, 0].reshape(1, -1)
        whole.append(part)
    out = compute(U, images[0], targets[0], pixel_mask[0], *whole)
    decoded, images_grad, loss = out[:3]
    pieces = []
    for g, w in zip(out[3:], shards):
        if w.ndim == 2:
            r, c = w.shape
            g = g.reshape(dp, r, fs, c).transpose(0, 2, 1, 3).reshape(dp, fs, r * c)
        else:
            g = jnp.broadcast_to(g.reshape(dp, 1, w.size), (dp, fs, w.size))
        pieces.append(g.astype(BF16))
    blocks = jnp.concatenate(pieces, axis=2).reshape(dp * fs, -1)
    arrived = lax.all_to_all(blocks, ("dp", "fsdp"), split_axis=0, concat_axis=0, tiled=True)
    total = arrived.astype(F32).sum(axis=0)
    grads, at = [], 0
    for w in shards:
        grads.append(total[at:at + w.size].reshape(w.shape))
        at += w.size
    grads = [grads[order.index(k)] for k in range(16)]
    return (decoded[None], images_grad[None], loss, *grads)


def solution(mesh):
    img, w, b = P(("dp", "fsdp"), None, None, None), P("dp", "fsdp"), P("dp")
    placed = (img, img, P(("dp", "fsdp"), None, None)) + (w,) * 4 + (b,) * 4 + (w,) * 4 + (b,) * 4
    return jax.shard_map(
        per_device, mesh=mesh, in_specs=placed,
        out_specs=(img, img, P(("dp", "fsdp"))) + (w,) * 4 + (b,) * 4 + (w,) * 4 + (b,) * 4,
        check_vma=False)
```

```python
import functools
import jax
import jax.numpy as jnp
from jax import lax
from jax.experimental import pallas as pl
from jax.experimental.pallas import tpu as pltpu
from jax.sharding import PartitionSpec as P

F32, BF16 = jnp.float32, jnp.bfloat16
MESH = pl.DeviceIdType.MESH


def dot(a, b):
    return jnp.dot(a, b, preferred_element_type=F32)


def dot_t(a, b):
    return lax.dot_general(a, b, (((1,), (1,)), ((), ())), preferred_element_type=F32)


def dot_p(a, b):
    return lax.dot_general(a, b, (((0,), (0,)), ((), ())), preferred_element_type=F32)


def loop(count, body, unroll):
    if unroll >= count:
        for c in range(count):
            body(c)
    else:
        def step(k, _):
            for u in range(unroll):
                body(k * unroll + u)
            return 0
        lax.fori_loop(0, count // unroll, step, 0)


def masks():
    lane = lax.broadcasted_iota(jnp.int32, (1, 1, 8, 128), 3)
    row = lax.broadcasted_iota(jnp.int32, (1, 1, 8, 128), 2)
    return lane < 64, row


def shifted(x):
    n = x.shape[0]
    _, row = masks()
    x4 = x.reshape(n, 8, 8, 128)
    nxt = jnp.where(row == 7, 0.0, pltpu.roll(x4[:, :1], 7, 2))
    prv = jnp.where(row == 0, 0.0, pltpu.roll(x4[:, 7:], 1, 2))
    up = jnp.concatenate([x4[:, 1:], nxt], axis=1)
    dn = jnp.concatenate([prv, x4[:, :7]], axis=1)
    return up, dn


def beside(x):
    lo, _ = masks()
    up, dn = shifted(x)
    return jnp.where(lo, up, dn).reshape(x.shape)


def folded(x):
    lo, _ = masks()
    up, dn = shifted(x)
    return jnp.where(lo, dn, up).reshape(x.shape)


def silu_parts(v):
    h = 0.5 * v
    u = 1.0 + jnp.tanh(h)
    act = h * u
    w = 0.5 * u
    return act, w + act * (1.0 - w)


def part_sum(x):
    return x.reshape(-1, 8, x.shape[-1]).sum(axis=0)


def put_pair(ref, idx, x):
    n = x.shape[0]
    ref[pl.ds(idx, n), :, 0:128] = x.astype(BF16)
    ref[pl.ds(idx, n), :, 128:256] = beside(x).astype(BF16)


def quad_rows(ref, r0, n, d):
    return jnp.concatenate([ref[2 * (r0 + k) + d] for k in range(n)], axis=0)


def split_rows(acc, n):
    a = acc.reshape(n, 1, 64, 256)
    return jnp.concatenate([a[..., :128], a[..., 128:]], axis=1).reshape(2 * n, 64, 128)


def stack_in(k):
    z = jnp.zeros_like(k[0])
    rows = ((k[1], k[2]), (k[0], k[1]), (z, k[0]), (k[2], z))
    return jnp.concatenate([jnp.concatenate(r, axis=1) for r in rows], axis=0)


def stack_out(k):
    z = jnp.zeros_like(k[0])
    rows = ((k[1], k[2], z, k[0]), (k[0], k[1], k[2], z))
    return jnp.concatenate([jnp.concatenate(r, axis=1) for r in rows], axis=0)


TAPS = ("ef", "es", "et", "df", "ds", "dt")
ROWS = dict(ef=2304, es=576, et=576, df=256, ds=576, dt=576, do=576)


def places(dp):
    enc, dec, at = {}, {}, 0
    for k in ("ef", "es", "et"):
        enc[k] = (at, ROWS[k] // dp)
        at += ROWS[k] // dp
    enc["extra"] = (at, 64)
    wide = at + 64
    at = 0
    for k in ("df", "ds", "dt"):
        dec[k] = (at, ROWS[k] // dp)
        at += ROWS[k] // dp
    for k in range(4):
        dec[k] = (at, ROWS["do"] // dp)
        at += ROWS["do"] // dp
    wide = max(wide, at)
    return enc, dec, wide + (-wide % 128)


def extra_block(eo, enc_row, dec_row):
    r = eo.shape[0]
    fill = lambda v: jnp.concatenate([v, jnp.zeros((1, 64 - v.shape[1]), F32)], axis=1)
    parts = [eo] + ([jnp.zeros((8 - r, 64), F32)] if r < 8 else [])
    return jnp.concatenate(parts + [fill(enc_row), fill(dec_row), jnp.zeros((6, 64), F32)], axis=0)


def lanes_to(parts, wide):
    at = sum(p.shape[1] for p in parts)
    if at < wide:
        parts = parts + [jnp.zeros((parts[0].shape[0], wide - at), parts[0].dtype)]
    return jnp.concatenate(parts, axis=1)


def where_am_i():
    a, b = lax.axis_index("dp"), lax.axis_index("fsdp")
    return a // 2, lax.rem(a, 2), b // 2, lax.rem(b, 2)


def device(z, y, x, c):
    return (z * 2 + y, x * 2 + c)


def far_copy(src, dst, send, recv, to):
    cp = pltpu.make_async_remote_copy(
        src_ref=src, dst_ref=dst, send_sem=send, recv_sem=recv, device_id=to, device_id_type=MESH)
    cp.start()
    return cp


def wait_all(copies):
    for cp in copies:
        cp.wait()


class Gather:
    def __init__(self, me, buf, send, recv):
        self.me, self.buf, self.send, self.recv = me, buf, send, recv
        self.nz = buf.shape[0]
        self.h = self.nz // 2

    def copy(self, view, k, to):
        return far_copy(view, view, self.send.at[k], self.recv.at[k], device(*to))

    def along_z(self):
        z, y, x, c = self.me
        mine = self.buf.at[z, y, x, c]
        self.fly = [self.copy(mine, 3 + k, (lax.rem(z + k, self.nz), y, x, c)) for k in range(1, self.nz)]

    def square_one(self):
        z, y, x, c = self.me
        wait_all(self.fly)
        lo, hi = pl.ds(0, self.h), pl.ds(self.h, self.nz - self.h)
        self.fly = [self.copy(self.buf.at[lo, y, x, c], 0, (z, 1 - y, x, c)),
                    self.copy(self.buf.at[hi, y, x, c], 1, (z, y, 1 - x, c))]

    def square_two(self):
        z, y, x, c = self.me
        wait_all(self.fly)
        lo, hi = pl.ds(0, self.h), pl.ds(self.h, self.nz - self.h)
        self.fly = [self.copy(self.buf.at[lo, :, x, c], 2, (z, y, 1 - x, c)),
                    self.copy(self.buf.at[hi, y, :, c], 3, (z, 1 - y, x, c))]

    def cores(self):
        z, y, x, c = self.me
        wait_all(self.fly)
        self.fly = [self.copy(self.buf.at[:, :, :, c], self.nz + 3, (z, y, x, 1 - c))]

    def finish(self):
        wait_all(self.fly)


def add16(p, q):
    return (p.astype(F32) + q.astype(F32)).astype(BF16)


class Scatter:
    def __init__(self, me, part, bufs, send, recv):
        self.me, self.part, self.send, self.recv = me, part, send, recv
        self.in1, self.s1, self.in2a, self.in2b, self.s2a, self.s2b, self.in3, self.s3, self.in4 = bufs
        self.nz = part.shape[0]
        self.h = self.nz // 2

    def copy(self, src, dst, k, to):
        return far_copy(src, dst, self.send.at[k], self.recv.at[k], device(*to))

    def cores(self):
        z, y, x, c = self.me
        self.fly = [self.copy(self.part.at[:, :, :, 1 - c], self.in1, 0, (z, y, x, 1 - c))]

    def square_one(self):
        z, y, x, c = self.me
        h, n = self.h, self.nz - self.h
        wait_all(self.fly)
        for k in range(self.nz):
            self.s1[k] = add16(self.part[k, :, :, c], self.in1[k])
        self.fly = [self.copy(self.s1.at[pl.ds(0, h), :, 1 - x], self.in2a, 1, (z, y, 1 - x, c)),
                    self.copy(self.s1.at[pl.ds(h, n), 1 - y], self.in2b, 2, (z, 1 - y, x, c))]

    def square_two(self):
        z, y, x, c = self.me
        h, n = self.h, self.nz - self.h
        wait_all(self.fly)
        for k in range(h):
            self.s2a[k] = add16(self.s1[k, :, x], self.in2a[k])
        for k in range(n):
            self.s2b[k] = add16(self.s1[h + k, y], self.in2b[k])
        self.fly = [self.copy(self.s2a.at[:, 1 - y], self.in3.at[pl.ds(0, h)], 3, (z, 1 - y, x, c)),
                    self.copy(self.s2b.at[:, 1 - x], self.in3.at[pl.ds(h, n)], 4, (z, y, 1 - x, c))]

    def along_z(self):
        z, y, x, c = self.me
        h, n = self.h, self.nz - self.h
        wait_all(self.fly)
        for k in range(h):
            self.s3[k] = add16(self.s2a[k, y], self.in3[k])
        for k in range(n):
            self.s3[h + k] = add16(self.s2b[k, x], self.in3[h + k])
        self.fly = []
        for k in range(1, self.nz):
            other = lax.rem(z + k, self.nz)
            self.fly.append(self.copy(self.s3.at[other], self.in4.at[k], 4 + k, (other, y, x, c)))

    def finish(self, out):
        z = self.me[0]
        wait_all(self.fly)
        total = self.s3[z].astype(F32)
        for k in range(1, self.nz):
            total = total + self.in4[k].astype(F32)
        out[...] = total


def main_kernel(U, *refs):
    (images_h, targets_h, mask_h, ef_h, es_h, et_h, eo_h, df_h, ds_h, dt_h, do_h, *rest) = refs
    biases_h, rest = rest[:8], rest[8:]
    (decoded_h, images_grad_h, loss, tot_e, tot_d,
     images, targets, mask, ef_s, es_s, et_s, eo_s, df_s, ds_s, dt_s, do_s, *rest) = rest
    biases_s, rest = rest[:8], rest[8:]
    (decoded, images_grad, src, act0, sl_src, z1, z2, a3, y1, y2, y3, s1, s2, s3, t1, t2, t3,
     mid, sl_mid, d0, g4, h4, zg, zh, stage,
     w_ef, w_es, w_et, v_es, v_et, w_ds, w_dt, v_ds, v_dt, w_do, w_eo, w_df, bias, bacc, eacc,
     whole_e, whole_d, part_e, part_d, *rest) = rest
    bufs_e, bufs_d, rest = rest[:9], rest[9:18], rest[18:]
    (shard_sem, image_sem, io_sem, ge_send, ge_recv, gd_send, gd_recv, se_send, se_recv, sd_send, sd_recv) = rest

    nz = whole_e.shape[0]
    dp = nz * 2
    enc_at, dec_at, wide = places(dp)
    me = where_am_i()
    z, y, x, c = me

    def near(src, dst, sem):
        cp = pltpu.make_async_copy(src, dst, sem)
        cp.start()
        return cp
    shards_h = (ef_h, es_h, et_h, eo_h, df_h, ds_h, dt_h, do_h, *biases_h)
    shards_s = (ef_s, es_s, et_s, eo_s, df_s, ds_s, dt_s, do_s, *biases_s)
    shard_copies = [near(p, q, shard_sem.at[k]) for k, (p, q) in enumerate(zip(shards_h, shards_s))]
    image_copies = [near(images_h.at[pl.ds(8 * k, 8)], images.at[pl.ds(8 * k, 8)], image_sem.at[k]) for k in range(4)]
    target_copy = near(targets_h, targets, io_sem.at[0])
    mask_copy = near(mask_h, mask, io_sem.at[1])

    barrier = pltpu.get_barrier_semaphore()
    others = [device(lax.rem(z + k, nz), y, x, c) for k in range(1, nz)]
    others += [device(z, 1 - y, x, c), device(z, y, 1 - x, c), device(z, y, x, 1 - c)]
    for d in others:
        pl.semaphore_signal(barrier, inc=1, device_id=d, device_id_type=MESH)
    wait_all(shard_copies)
    enc_row = jnp.concatenate([b[...].astype(F32) for b in biases_s[:4]], axis=1)
    dec_row = jnp.concatenate([b[...].astype(F32) for b in biases_s[4:]], axis=1)
    extra = extra_block(eo_s[...].astype(F32), enc_row, dec_row).astype(BF16)
    whole_e[z, y, x, c] = lanes_to([ef_s[...], es_s[...], et_s[...], extra], wide)
    whole_d[z, y, x, c] = lanes_to([df_s[...], ds_s[...], dt_s[...]] + [do_s[16 * k:16 * k + 16] for k in range(4)], wide)
    pl.semaphore_wait(barrier, len(others))
    ge = Gather(me, whole_e, ge_send, ge_recv)
    gd = Gather(me, whole_d, gd_send, gd_recv)
    ge.along_z()
    gd.along_z()

    for ref in (act0, g4, z1, z2, y1, y2, y3, zg, zh):
        ref[0] = jnp.zeros(ref.shape[1:], ref.dtype)
        ref[33] = jnp.zeros(ref.shape[1:], ref.dtype)
    bacc[...] = jnp.zeros_like(bacc)
    eacc[...] = jnp.zeros_like(eacc)

    def across(whole, place):
        at, n = place
        return jnp.concatenate([
            jnp.concatenate([whole[a // 2, a % 2, b // 2, b % 2, :, at:at + n] for b in range(4)], axis=0)
            for a in range(dp)], axis=1)

    def tap(k, i, n):
        return [k[:, (3 * i + j) * n:(3 * i + j + 1) * n] for j in range(3)]

    def quad_weights(k, w_ref, v_ref):
        w_ref[0, 128:256, :] = jnp.zeros((128, 256), BF16)
        w_ref[3, 0:128, :] = jnp.zeros((128, 256), BF16)
        v_ref[0, :, 128:256] = jnp.zeros((256, 128), BF16)
        v_ref[3, :, 0:128] = jnp.zeros((256, 128), BF16)
        for i in range(3):
            t = tap(k, i, 64)
            f = stack_out(t)
            w_ref[i, 0:128, :] = f
            w_ref[i + 1, 128:256, :] = f
            b = stack_in(t)
            v_ref[2 - i, :, 0:128] = b
            v_ref[3 - i, :, 128:256] = b

    def two(k):
        z = jnp.zeros_like(k)
        return jnp.concatenate([jnp.concatenate([k, z], axis=1), jnp.concatenate([z, k], axis=1)], axis=0)

    r_eo = 64 // dp
    b_at = [(0, 64 // dp), (64 // dp, 64 // dp), (128 // dp, 64 // dp), (192 // dp, 256 // dp)]

    def encoder_weights():
        k = across(whole_e, enc_at["ef"])
        for i in range(3):
            w_ef[i] = stack_in(tap(k, i, 256))
        quad_weights(across(whole_e, enc_at["es"]), w_es, v_es)
        quad_weights(across(whole_e, enc_at["et"]), w_et, v_et)
        at, n = enc_at["extra"]
        blocks = [[whole_e[a // 2, a % 2, b // 2, b % 2, :, at:at + n].astype(F32) for b in range(4)] for a in range(dp)]
        w_eo[...] = two(jnp.concatenate([
            jnp.concatenate([blk[0:r_eo] for blk in blocks[a]], axis=1) for a in range(dp)], axis=0).astype(BF16))
        for row in range(2):
            for k, (at, size) in enumerate(b_at):
                v = jnp.concatenate([blocks[a][0][8 + row:9 + row, at:at + size] for a in range(dp)], axis=1)
                v = jnp.concatenate([v, v], axis=1)
                if k < 3:
                    bias[3 * row + k, :, 0:128] = v
                else:
                    bias[6 + row] = v * (1.0 / 64.0)

    def decoder_weights():
        w_df[...] = two(across(whole_d, dec_at["df"]))
        quad_weights(across(whole_d, dec_at["ds"]), w_ds, v_ds)
        quad_weights(across(whole_d, dec_at["dt"]), w_dt, v_dt)
        quarter = [across(whole_d, dec_at[k]) for k in range(4)]
        k = jnp.concatenate([quarter[k][16 * b:16 * b + 16] for b in range(4) for k in range(4)], axis=0)
        for i in range(3):
            w_do[i] = stack_out(tap(k, i, 64))

    def to_pairs(v, slot):
        stage[slot, 0] = v[:, :128]
        stage[slot, 1] = v[:, 128:]
        return [jnp.concatenate([stage[slot, h, pl.ds(2 * t + e, 8, stride=16), :] for t in range(8)], axis=0)
                for e in range(2) for h in range(2)]

    def to_natural(v, slot):
        for e in range(2):
            for h in range(2):
                for t in range(8):
                    stage[slot, h, pl.ds(2 * t + e, 8, stride=16), :] = v[8 * t:8 * t + 8, e * 256 + h * 128:e * 256 + h * 128 + 128]
        return stage[slot, 0], stage[slot, 1]

    def body_b(p):
        v = images[p].astype(F32)
        slot = p % 4 if isinstance(p, int) else lax.rem(p, 4)
        parts = to_pairs(v, slot)
        for q, x in enumerate(parts):
            ln = slice(q * 128, q * 128 + 128)
            act, slope = silu_parts(x)
            src[p, :, ln] = x.astype(BF16)
            act0[p + 1, :, ln] = act.astype(BF16)
            sl_src[p, :, ln] = slope
    def rows_b(k):
        image_copies[k].wait()
        loop(8, lambda r: body_b(8 * k + r), U['B'])
    rows_b(0)
    ge.square_one()
    rows_b(1)
    ge.square_two()
    rows_b(2)
    ge.cores()
    gd.square_one()
    rows_b(3)
    ge.finish()
    encoder_weights()

    def hidden(pre, b, slope_ref, row):
        act, slope = silu_parts(pre + bias[b, :, 0:128])
        slope_ref[pl.ds(row, pre.shape[0])] = slope
        return act

    n = U['nC']
    def body(c):
        p = c * n
        acc = 0.0
        for i in range(3):
            acc = acc + dot_t(act0[pl.ds(p + i, n)].reshape(n * 64, 512), w_ef[i])
        acc = acc.reshape(n, 64, 256)
        pre = acc[..., :128] + folded(acc[..., 128:])
        put_pair(z1, p + 1, hidden(pre, 0, s1, p))
    loop(32 // n, body, U['C'])

    def quad_conv(zin, w, b, slope_ref, zout, n, unroll, pair=True):
        def body(c):
            acc = 0.0
            for d in range(4):
                acc = acc + dot_t(quad_rows(zin, c * n, n, d), w[d])
            act = hidden(split_rows(acc, n), b, slope_ref, c * 2 * n)
            if pair:
                put_pair(zout, c * 2 * n + 1, act)
            else:
                zout[pl.ds(c * 2 * n, 2 * n)] = act.astype(BF16)
        loop(16 // n, body, unroll)

    gd.square_two()
    quad_conv(z1, w_es, 1, s2, z2, U['nQ'], U['Q'])
    gd.cores()
    quad_conv(z2, w_et, 2, s3, a3, U['nQ'], U['Q'], pair=False)

    gd.finish()
    decoder_weights()

    n = U['nF']
    def body(c):
        p = c * n
        br = dot(a3[pl.ds(p, n)].reshape(n * 64, 128), w_eo[...])
        m = src[pl.ds(p, n)].astype(F32).reshape(n * 64, 512) + (br * (1.0 / 64.0) + bias[6])
        act, slope = silu_parts(m)
        mid[pl.ds(p, n)] = m.reshape(n, 64, 512)
        sl_mid[pl.ds(p, n)] = slope.reshape(n, 64, 512)
        act = act.astype(BF16)
        d0[pl.ds(p, n)] = act.reshape(n, 64, 512)
        pre = dot_t(act, w_df[...]).reshape(n, 64, 128)
        put_pair(y1, p + 1, hidden(pre, 3, t1, p))
    loop(32 // n, body, U['F'])

    quad_conv(y1, w_ds, 4, t2, y2, U['nQ'], U['Q'])
    quad_conv(y2, w_dt, 5, t3, y3, U['nQ'], U['Q'])

    mask_copy.wait()
    target_copy.wait()
    mk = mask[...].astype(F32)
    tall = jnp.sum(mk[:, 0:1])
    broad = jnp.sum(mk[0:1, :])
    sub = lax.broadcasted_iota(jnp.int32, (64, 128), 0)
    column = lax.rem(sub, 8) * 16 + 2 * (sub // 8)
    wi = broad.astype(jnp.int32)
    hi = tall.astype(jnp.int32)
    col_mask = [jnp.where(column + e < wi, 1.0, 0.0) for e in range(2)]
    n = U['nJ']
    def body(c):
        p = c * n
        acc = 0.0
        for i in range(3):
            acc = acc + dot_t(y3[pl.ds(p + i, n)].reshape(n * 64, 256), w_do[i])
        acc = acc.reshape(n, 64, 512)
        for r in range(n):
            m = mid[p + r]
            res = m + (acc[r] * (1.0 / 64.0) + bias[7])
            slot = r % 2
            a, b = to_natural(res, 2 + slot)
            decoded[p + r, :, 0:128] = a.astype(BF16)
            decoded[p + r, :, 128:256] = b.astype(BF16)
            t = to_pairs(targets[p + r].astype(F32), slot)
            row_on = jnp.where(p + r < hi, 1.0, 0.0)
            for q in range(4):
                ln = slice(q * 128, q * 128 + 128)
                diff = res[:, ln] - t[q]
                g = diff * (col_mask[q // 2] * row_on)
                mid[p + r, :, ln] = g
                eacc[...] += part_sum(g * diff)
                g = g * (1.0 / 64.0)
                g4[p + r + 1, :, ln] = g.astype(BF16)
                bacc[7, :, ln] += part_sum(g)
    loop(32 // n, body, U['J'])
    decoded_copy = near(decoded, decoded_h, io_sem.at[2])
    loss[0] = 0.5 * jnp.sum(eacc[...]) / (tall * broad * 256.0)

    def back(x, slope_ref, row, b):
        g = x * slope_ref[pl.ds(row, x.shape[0])]
        bacc[b, :, 0:128] += part_sum(g)
        return g

    n = U['nC']
    def body(c):
        p = c * n
        acc = 0.0
        for i in range(3):
            acc = acc + dot(g4[pl.ds(p + i, n)].reshape(n * 64, 512), w_do[2 - i])
        acc = acc.reshape(n, 64, 256)
        x = acc[..., :128] + folded(acc[..., 128:])
        put_pair(zg, p + 1, back(x, t3, p, 5))
    loop(32 // n, body, U['K'])

    M = [3, 0, 1, 2]

    gv = g4[pl.ds(1, 32)].reshape(2048, 512)
    cols = []
    for i in range(3):
        t = dot_p(gv, y3[pl.ds(i, 32)].reshape(2048, 256))
        for j in range(3):
            a, b = M[j] * 64, M[j + 1] * 64
            cols.append(t[0:256, a:a + 64] + t[256:512, b:b + 64])
    k_do = jnp.concatenate(cols, axis=1).astype(BF16)
    for a in range(dp):
        n = 576 // dp
        v = k_do[:, n * a:n * a + n]
        for b in range(4):
            for k in range(4):
                at = dec_at[k][0]
                r = 64 * b + 16 * k
                part_d[a // 2, a % 2, b // 2, b % 2, :, at:at + n] = v[r:r + 16]

    def deal(part, place, k):
        at, n = place
        k = k.astype(BF16)
        for a in range(dp):
            v = k[:, n * a:n * a + n]
            for b in range(4):
                part[a // 2, a % 2, b // 2, b % 2, :, at:at + n] = v[16 * b:16 * b + 16]

    def quad_wgrad(z, g_ref, part, place):
        gq = jnp.concatenate([
            jnp.concatenate([g_ref[2 * r + 1, :, 0:128] for r in range(16)], axis=0),
            jnp.concatenate([g_ref[2 * r + 2, :, 0:128] for r in range(16)], axis=0)], axis=1)
        t = [dot_p(gq, quad_rows(z, 0, 16, d)) for d in range(4)]
        cols = []
        for i in range(3):
            s = t[i][0:128] + t[i + 1][128:256]
            for j in range(3):
                a, b = M[j] * 64, M[j + 1] * 64
                cols.append(s[0:64, a:a + 64] + s[64:128, b:b + 64])
        deal(part, place, jnp.concatenate(cols, axis=1))

    def quad_back(zin, v, slope_ref, b, zout, n, unroll):
        def body(c):
            acc = 0.0
            for d in range(4):
                acc = acc + dot(quad_rows(zin, c * n, n, d), v[d])
            put_pair(zout, c * 2 * n + 1, back(split_rows(acc, n), slope_ref, c * 2 * n, b))
        loop(16 // n, body, unroll)

    quad_back(zg, v_dt, t2, 4, zh, U['nQ'], U['Q'])
    quad_wgrad(y2, zg, part_d, dec_at["dt"])
    quad_back(zh, v_ds, t1, 3, zg, U['nQ'], U['Q'])
    quad_wgrad(y1, zh, part_d, dec_at["ds"])

    t = dot_p(zg[pl.ds(1, 32), :, 0:128].reshape(2048, 128), d0[...].reshape(2048, 512))
    deal(part_d, dec_at["df"], t[0:64, 0:256] + t[64:128, 256:512])
    sd = Scatter(me, part_d, bufs_d, sd_send, sd_recv)
    sd.cores()

    n = U['nF']
    def body(c):
        p = c * n
        bk = dot(zg[pl.ds(p + 1, n), :, 0:128].reshape(n * 64, 128), w_df[...])
        gm = mid[pl.ds(p, n)].reshape(n * 64, 512) + sl_mid[pl.ds(p, n)].reshape(n * 64, 512) * bk
        mid[pl.ds(p, n)] = gm.reshape(n, 64, 512)
        g = gm * (1.0 / 64.0)
        bacc[6] += part_sum(g)
        g = g.astype(BF16)
        h4[pl.ds(p, n)] = g.reshape(n, 64, 512)
        x = dot_t(g, w_eo[...]).reshape(n, 64, 128)
        put_pair(zh, p + 1, back(x, s3, p, 2))
    loop(32 // n, body, U['F'])

    sd.square_one()

    t = dot_p(a3[...].reshape(2048, 128), h4[...].reshape(2048, 512))
    k_eo = t[0:64, 0:256] + t[64:128, 256:512]

    quad_back(zh, v_et, s2, 1, zg, U['nQ'], U['Q'])
    sd.square_two()
    quad_wgrad(z2, zh, part_e, enc_at["et"])
    sd.along_z()
    quad_back(zg, v_es, s1, 0, zh, U['nQ'], U['Q'])
    quad_wgrad(z1, zg, part_e, enc_at["es"])

    gv = zh[pl.ds(1, 32)].reshape(2048, 256)
    cols = []
    for i in range(3):
        t = dot_p(gv, act0[pl.ds(i, 32)].reshape(2048, 512))
        cols.append(t[64:128, 0:256] + t[128:192, 256:512])
        cols.append(t[0:64, 0:256] + t[64:128, 256:512])
        cols.append(t[192:256, 0:256] + t[0:64, 256:512])
    deal(part_e, enc_at["ef"], jnp.concatenate(cols, axis=1))
    sd.finish(tot_d)

    sums = []
    for n in range(8):
        v = jnp.sum(bacc[n], axis=0, keepdims=True)
        sums.append(v[:, 0:256] + v[:, 256:512] if n >= 6 else v[:, 0:64] + v[:, 64:128])
    at = enc_at["extra"][0]
    for a in range(dp):
        rows = []
        for group in ((0, 1, 2, 6), (3, 4, 5, 7)):
            rows.append(jnp.concatenate([sums[k][:, a * n:a * n + n] for k, (_, n) in zip(group, b_at)], axis=1))
        for b in range(4):
            extra = extra_block(k_eo[a * r_eo:a * r_eo + r_eo, 64 * b:64 * b + 64], *rows)
            part_e[a // 2, a % 2, b // 2, b % 2, :, at:at + 64] = extra.astype(BF16)
    se = Scatter(me, part_e, bufs_e, se_send, se_recv)
    se.cores()

    n = U['nJ']
    def body_q(c):
        p = c * n
        acc = 0.0
        for i in range(3):
            acc = acc + dot(zh[pl.ds(p + i, n)].reshape(n * 64, 256), w_ef[2 - i])
        acc = acc.reshape(n, 64, 512)
        for r in range(n):
            g = mid[p + r] + sl_src[p + r] * acc[r]
            a, b = to_natural(g, r % 4)
            images_grad[p + r, :, 0:128] = a.astype(BF16)
            images_grad[p + r, :, 128:256] = b.astype(BF16)
    grad_copies = []

    def rows_q(k):
        loop(8 // n, lambda r: body_q(k * (8 // n) + r), U['Qr'])
        grad_copies.append(near(images_grad.at[pl.ds(8 * k, 8)], images_grad_h.at[pl.ds(8 * k, 8)], image_sem.at[k]))
    rows_q(0)
    se.square_one()
    rows_q(1)
    se.square_two()
    rows_q(2)
    se.along_z()
    rows_q(3)
    se.finish(tot_e)
    decoded_copy.wait()
    wait_all(grad_copies)


def last_kernel(decoded_i, images_grad_i, loss_i, tot_e, tot_d, decoded, images_grad, loss, *refs):
    g_ef, g_es, g_et, g_eo, g_df, g_ds, g_dt, g_do = refs[:8]
    biases, hold, sem = refs[8:16], refs[16], refs[17]
    dp = 64 // g_eo.shape[0]
    pairs = [(p, q, n * 4 + k, pl.ds(8 * k, 8)) for k in range(4) for n, (p, q) in enumerate(((decoded_i, decoded), (images_grad_i, images_grad)))]
    ins = [pltpu.make_async_copy(p.at[rows], hold.at[k], sem.at[k]) for p, q, k, rows in pairs]
    outs = [pltpu.make_async_copy(hold.at[k], q.at[rows], sem.at[8 + k]) for p, q, k, rows in pairs]
    for cp in ins:
        cp.start()
    loss[0] = loss_i[0]
    enc_at, dec_at, wide = places(dp)
    e, d = tot_e[...], tot_d[...]
    for k, ref in (("ef", g_ef), ("es", g_es), ("et", g_et)):
        at, n = enc_at[k]
        ref[...] = e[:, at:at + n]
    for k, ref in (("df", g_df), ("ds", g_ds), ("dt", g_dt)):
        at, n = dec_at[k]
        ref[...] = d[:, at:at + n]
    for k in range(4):
        at, n = dec_at[k]
        g_do[16 * k:16 * k + 16] = d[:, at:at + n]
    at = enc_at["extra"][0]
    g_eo[...] = e[0:64 // dp, at:at + 64]
    for row in range(2):
        off = at
        for k in range(4):
            n = (64, 64, 64, 256)[k] // dp
            biases[4 * row + k][...] = e[8 + row:9 + row, off:off + n]
            off += n
    for p, q in zip(ins, outs):
        p.wait()
        q.start()
    wait_all(outs)


U = dict(B=4, nC=8, C=1, K=1, nQ=8, Q=1, nF=4, F=1, nJ=4, J=1, Qr=1)


def per_device(images, targets, pixel_mask, ef, es, et, eo, eba, ebb, ebc, ebd, df, ds, dt, do, dba, dbb, dbc, dbd):
    dp = lax.axis_size("dp")
    nz = dp // 2
    h = nz // 2
    wide = places(dp)[2]
    vm = pl.BlockSpec(memory_space=pltpu.VMEM)
    far = pl.BlockSpec(memory_space=pl.ANY)
    smem = pl.BlockSpec(memory_space=pltpu.SMEM)
    sem = pltpu.SemaphoreType.DMA
    V = lambda shape, dt: pltpu.VMEM(shape, dt)
    S = jax.ShapeDtypeStruct
    args = [images[0], targets[0], pixel_mask[0], ef.T, es.T, et.T, eo, df.T, ds.T, dt.T, do.T]
    args += [b.reshape(1, -1) for b in (eba, ebb, ebc, ebd, dba, dbb, dbc, dbd)]
    comm = [V((nz, 2, 2, 16, wide), BF16), V((nz, 2, 2, 16, wide), BF16), V((h, 2, 16, wide), BF16), V((nz - h, 2, 16, wide), BF16),
            V((h, 2, 16, wide), BF16), V((nz - h, 2, 16, wide), BF16), V((nz, 16, wide), BF16), V((nz, 16, wide), BF16),
            V((nz, 16, wide), BF16)]
    big = S((32, 128, 256), BF16)
    tot = S((16, wide), F32)
    decoded, images_grad, loss, tot_e, tot_d = pl.pallas_call(
        functools.partial(main_kernel, U),
        out_shape=[big, big, S((1,), F32), tot, tot],
        in_specs=[far] * 19, out_specs=[far, far, smem, vm, vm],
        scratch_shapes=[V(a.shape, a.dtype) for a in args] + [
            V((32, 128, 256), BF16), V((32, 128, 256), BF16),
            V((32, 64, 512), BF16), V((34, 64, 512), BF16), V((32, 64, 512), F32),
            V((34, 64, 256), BF16), V((34, 64, 256), BF16), V((32, 64, 128), BF16),
            V((34, 64, 256), BF16), V((34, 64, 256), BF16), V((34, 64, 256), BF16)] + [V((32, 64, 128), F32)] * 6 + [
            V((32, 64, 512), F32), V((32, 64, 512), F32), V((32, 64, 512), BF16),
            V((34, 64, 512), BF16), V((32, 64, 512), BF16), V((34, 64, 256), BF16), V((34, 64, 256), BF16),
            V((4, 2, 128, 128), F32),
            V((3, 256, 512), BF16)] + [V((4, 256, 256), BF16)] * 8 + [
            V((3, 512, 256), BF16), V((128, 512), BF16), V((128, 512), BF16),
            V((8, 1, 512), F32), V((8, 8, 512), F32), V((8, 128), F32)]
        + [V((nz, 2, 2, 2, 16, wide), BF16)] * 4 + comm * 2
        + [sem((16,)), sem((4,)), sem((3,))] + [sem((nz + 4,))] * 8,
        compiler_params=pltpu.CompilerParams(collective_id=0, has_side_effects=True, vmem_limit_bytes=63 * 2**20),
    )(*args)
    f = lambda *s: S(s, F32)
    outs = pl.pallas_call(
        last_kernel,
        out_shape=[big, big, S((1,), F32), f(16, 2304 // dp), f(16, 576 // dp), f(16, 576 // dp), f(64 // dp, 64), f(16, 256 // dp),
                   f(16, 576 // dp), f(16, 576 // dp), f(64, 576 // dp)] + [f(1, s // dp) for s in (64, 64, 64, 256) * 2],
        in_specs=[far, far, smem, vm, vm], out_specs=[far, far, smem] + [vm] * 16, scratch_shapes=[V((8, 8, 128, 256), BF16), sem((16,))],
        compiler_params=pltpu.CompilerParams(vmem_limit_bytes=60 * 2**20),
    )(decoded, images_grad, loss, tot_e, tot_d)
    decoded, images_grad, loss, g_ef, g_es, g_et, g_eo, g_df, g_ds, g_dt, g_do = outs[:11]
    bs = [b.reshape(-1) for b in outs[11:]]
    return (decoded[None], images_grad[None], loss, g_ef.T, g_es.T, g_et.T, g_eo, *bs[:4],
            g_df.T, g_ds.T, g_dt.T, g_do.T, *bs[4:])


def solution(mesh):
    img, w, b = P(("dp", "fsdp"), None, None, None), P("dp", "fsdp"), P("dp")
    placed = (img, img, P(("dp", "fsdp"), None, None)) + (w,) * 4 + (b,) * 4 + (w,) * 4 + (b,) * 4
    return jax.shard_map(
        per_device, mesh=mesh, in_specs=placed,
        out_specs=(img, img, P(("dp", "fsdp"))) + (w,) * 4 + (b,) * 4 + (w,) * 4 + (b,) * 4,
        check_vma=False)
```

```python
import functools
import jax
import jax.numpy as jnp
from jax import lax
from jax.experimental import pallas as pl
from jax.experimental.pallas import tpu as pltpu
from jax.sharding import PartitionSpec as P

F32, BF16 = jnp.float32, jnp.bfloat16
MESH = pl.DeviceIdType.MESH


def dot(a, b):
    return jnp.dot(a, b, preferred_element_type=F32)


def dot_t(a, b):
    return lax.dot_general(a, b, (((1,), (1,)), ((), ())), preferred_element_type=F32)


def dot_p(a, b):
    return lax.dot_general(a, b, (((0,), (0,)), ((), ())), preferred_element_type=F32)


def loop(count, body, unroll):
    if unroll >= count:
        for c in range(count):
            body(c)
    else:
        def step(k, _):
            for u in range(unroll):
                body(k * unroll + u)
            return 0
        lax.fori_loop(0, count // unroll, step, 0)


def masks():
    lane = lax.broadcasted_iota(jnp.int32, (1, 1, 8, 128), 3)
    row = lax.broadcasted_iota(jnp.int32, (1, 1, 8, 128), 2)
    return lane < 64, row


def shifted(x):
    n = x.shape[0]
    _, row = masks()
    x4 = x.reshape(n, 8, 8, 128)
    nxt = jnp.where(row == 7, 0.0, pltpu.roll(x4[:, :1], 7, 2))
    prv = jnp.where(row == 0, 0.0, pltpu.roll(x4[:, 7:], 1, 2))
    up = jnp.concatenate([x4[:, 1:], nxt], axis=1)
    dn = jnp.concatenate([prv, x4[:, :7]], axis=1)
    return up, dn


def beside(x):
    lo, _ = masks()
    up, dn = shifted(x)
    return jnp.where(lo, up, dn).reshape(x.shape)


def folded(x):
    lo, _ = masks()
    up, dn = shifted(x)
    return jnp.where(lo, dn, up).reshape(x.shape)


def silu_parts(v):
    h = 0.5 * v
    u = 1.0 + jnp.tanh(h)
    act = h * u
    w = 0.5 * u
    return act, w + act * (1.0 - w)


def part_sum(x):
    return x.reshape(-1, 8, x.shape[-1]).sum(axis=0)


def put_pair(ref, idx, x):
    ref[idx, :, 0:128] = x.astype(BF16)
    ref[idx, :, 128:256] = beside(x[None])[0].astype(BF16)


def quad_rows(ref, r0, n, d):
    return jnp.concatenate([ref[2 * (r0 + k) + d] for k in range(n)], axis=0)


def rows_of(x, n):
    return [x[64 * r:64 * r + 64] for r in range(n)]


def stack_in(k):
    z = jnp.zeros_like(k[0])
    rows = ((k[1], k[2]), (k[0], k[1]), (z, k[0]), (k[2], z))
    return jnp.concatenate([jnp.concatenate(r, axis=1) for r in rows], axis=0)


def stack_out(k):
    z = jnp.zeros_like(k[0])
    rows = ((k[1], k[2], z, k[0]), (k[0], k[1], k[2], z))
    return jnp.concatenate([jnp.concatenate(r, axis=1) for r in rows], axis=0)


TAPS = ("ef", "es", "et", "df", "ds", "dt")
ROWS = dict(ef=2304, es=576, et=576, df=256, ds=576, dt=576, do=576)


def places(dp):
    groups = ((("ef", 2304 // dp), ("es", 576 // dp), ("bias", 128 // dp)),
              (("et", 576 // dp), ("df", 256 // dp), ("eo", 64)),
              (("ds", 576 // dp), ("dt", 576 // dp)) + tuple((k, 576 // dp) for k in range(4)))
    spots, widths = {}, []
    for g, group in enumerate(groups):
        at = 0
        for name, n in group:
            spots[name] = (g, at, n)
            at += n
        widths.append(at + (-at % 128))
    return spots, widths


def bias_block(parts):
    w = parts[3].shape[1] // 2
    n = parts[0].shape[1]
    fill = lambda v: jnp.concatenate([v, jnp.zeros((1, w - n), F32)], axis=1)
    rows = [fill(parts[k]) for k in (0, 1, 2, 4, 5, 6)]
    for k in (3, 7):
        rows += [parts[k][:, :w], parts[k][:, w:]]
    return jnp.concatenate(rows + [jnp.zeros((6, w), F32)], axis=0)


def bias_rows(block, n):
    thin = [block[k:k + 1, :n] for k in range(6)]
    wide = [jnp.concatenate([block[k:k + 1], block[k + 1:k + 2]], axis=1) for k in (6, 8)]
    return thin[:3] + wide[:1] + thin[3:] + wide[1:]


def eo_block(eo):
    return jnp.concatenate([eo, jnp.zeros((16 - eo.shape[0], 64), F32)], axis=0)


def lanes_to(parts, wide):
    at = sum(p.shape[1] for p in parts)
    if at < wide:
        parts = parts + [jnp.zeros((parts[0].shape[0], wide - at), parts[0].dtype)]
    return jnp.concatenate(parts, axis=1)


def where_am_i():
    a, b = lax.axis_index("dp"), lax.axis_index("fsdp")
    return a // 2, lax.rem(a, 2), b // 2, lax.rem(b, 2)


def device(z, y, x, c):
    return (z * 2 + y, x * 2 + c)


def far_copy(src, dst, send, recv, to):
    cp = pltpu.make_async_remote_copy(
        src_ref=src, dst_ref=dst, send_sem=send, recv_sem=recv, device_id=to, device_id_type=MESH)
    cp.start()
    return cp


def wait_all(copies):
    for cp in copies:
        cp.wait()


class Gather:
    def __init__(self, me, buf, send, recv):
        self.me, self.buf, self.send, self.recv = me, buf, send, recv
        self.nz = buf.shape[0]
        self.h = self.nz // 2

    def copy(self, view, k, to):
        return far_copy(view, view, self.send.at[k], self.recv.at[k], device(*to))

    def along_z(self):
        z, y, x, c = self.me
        mine = self.buf.at[z, y, x, c]
        self.fly = [self.copy(mine, 3 + k, (lax.rem(z + k, self.nz), y, x, c)) for k in range(1, self.nz)]

    def square_one(self):
        z, y, x, c = self.me
        wait_all(self.fly)
        lo, hi = pl.ds(0, self.h), pl.ds(self.h, self.nz - self.h)
        self.fly = [self.copy(self.buf.at[lo, y, x, c], 0, (z, 1 - y, x, c)),
                    self.copy(self.buf.at[hi, y, x, c], 1, (z, y, 1 - x, c))]

    def square_two(self):
        z, y, x, c = self.me
        wait_all(self.fly)
        lo, hi = pl.ds(0, self.h), pl.ds(self.h, self.nz - self.h)
        self.fly = [self.copy(self.buf.at[lo, :, x, c], 2, (z, y, 1 - x, c)),
                    self.copy(self.buf.at[hi, y, :, c], 3, (z, 1 - y, x, c))]

    def cores(self):
        z, y, x, c = self.me
        wait_all(self.fly)
        self.fly = [self.copy(self.buf.at[:, :, :, c], self.nz + 3, (z, y, x, 1 - c))]

    def finish(self):
        wait_all(self.fly)


class DirectGather:
    def __init__(self, me, buf, send, recv):
        self.me, self.buf, self.send, self.recv = me, buf, send, recv
        self.nz = buf.shape[0]
        self.steps = chip_steps(self.nz)

    def copy(self, view, k, to):
        return far_copy(view, view, self.send.at[k], self.recv.at[k], device(*to))

    def chips(self):
        z, y, x, c = self.me
        mine = self.buf.at[z, y, x, c]
        self.fly = {}
        for k, step in reversed(list(enumerate(self.steps))):
            self.fly[k] = self.copy(mine, k, other_chip(self.me, step, self.nz))

    def cores(self):
        z, y, x, c = self.me
        self.last = []
        for dz in range(self.nz):
            wait_all([self.fly[k] for k, step in enumerate(self.steps) if step[0] == dz])
            rows = self.buf.at[lax.rem(z + self.nz - dz, self.nz), :, :, c]
            self.last.append(self.copy(rows, len(self.steps) + dz, (z, y, x, 1 - c)))

    def finish(self):
        wait_all(self.last)


class DirectScatter:
    def __init__(self, me, part, bufs, send, recv):
        self.me, self.part, self.send, self.recv = me, part, send, recv
        self.in1, self.s1, self.in2 = bufs
        self.nz = part.shape[0]
        self.steps = chip_steps(self.nz)

    def copy(self, src, dst, k, to):
        return far_copy(src, dst, self.send.at[k], self.recv.at[k], device(*to))

    def cores(self):
        z, y, x, c = self.me
        self.fly = [self.copy(self.part.at[:, :, :, 1 - c], self.in1, len(self.steps), (z, y, x, 1 - c))]

    def chips(self):
        z, y, x, c = self.me
        wait_all(self.fly)
        for k in range(self.nz):
            self.s1[k] = add16(self.part[k, :, :, c], self.in1[k])
        self.fly = []
        for k, step in reversed(list(enumerate(self.steps))):
            to = other_chip(self.me, step, self.nz)
            self.fly.append(self.copy(self.s1.at[to[0], to[1], to[2]], self.in2.at[k], k, to))

    def finish(self, out):
        z, y, x, c = self.me
        wait_all(self.fly)
        total = self.s1[z, y, x].astype(F32)
        for k in range(len(self.steps)):
            total = total + self.in2[k].astype(F32)
        out[...] = total


def chip_steps(nz):
    return [(dz, dy, dx) for dz in range(nz) for dy in range(2) for dx in range(2)][1:]


def other_chip(me, step, nz):
    z, y, x, c = me
    return (lax.rem(z + step[0], nz), lax.rem(y + step[1], 2), lax.rem(x + step[2], 2), c)


def add16(p, q):
    return (p.astype(F32) + q.astype(F32)).astype(BF16)


class Scatter:
    def __init__(self, me, part, bufs, send, recv):
        self.me, self.part, self.send, self.recv = me, part, send, recv
        self.in1, self.s1, self.in2a, self.in2b, self.s2a, self.s2b, self.in3, self.s3, self.in4 = bufs
        self.nz = part.shape[0]
        self.h = self.nz // 2

    def copy(self, src, dst, k, to):
        return far_copy(src, dst, self.send.at[k], self.recv.at[k], device(*to))

    def cores(self):
        z, y, x, c = self.me
        self.fly = [self.copy(self.part.at[:, :, :, 1 - c], self.in1, 0, (z, y, x, 1 - c))]

    def square_one(self):
        z, y, x, c = self.me
        h, n = self.h, self.nz - self.h
        wait_all(self.fly)
        for k in range(self.nz):
            self.s1[k] = add16(self.part[k, :, :, c], self.in1[k])
        self.fly = [self.copy(self.s1.at[pl.ds(0, h), :, 1 - x], self.in2a, 1, (z, y, 1 - x, c)),
                    self.copy(self.s1.at[pl.ds(h, n), 1 - y], self.in2b, 2, (z, 1 - y, x, c))]

    def square_two(self):
        z, y, x, c = self.me
        h, n = self.h, self.nz - self.h
        wait_all(self.fly)
        for k in range(h):
            self.s2a[k] = add16(self.s1[k, :, x], self.in2a[k])
        for k in range(n):
            self.s2b[k] = add16(self.s1[h + k, y], self.in2b[k])
        self.fly = [self.copy(self.s2a.at[:, 1 - y], self.in3.at[pl.ds(0, h)], 3, (z, 1 - y, x, c)),
                    self.copy(self.s2b.at[:, 1 - x], self.in3.at[pl.ds(h, n)], 4, (z, y, 1 - x, c))]

    def along_z(self):
        z, y, x, c = self.me
        h, n = self.h, self.nz - self.h
        wait_all(self.fly)
        for k in range(h):
            self.s3[k] = add16(self.s2a[k, y], self.in3[k])
        for k in range(n):
            self.s3[h + k] = add16(self.s2b[k, x], self.in3[h + k])
        self.fly = []
        for k in range(1, self.nz):
            other = lax.rem(z + k, self.nz)
            self.fly.append(self.copy(self.s3.at[other], self.in4.at[k], 4 + k, (other, y, x, c)))

    def finish(self, out):
        z = self.me[0]
        wait_all(self.fly)
        total = self.s3[z].astype(F32)
        for k in range(1, self.nz):
            total = total + self.in4[k].astype(F32)
        out[...] = total


def main_kernel(U, *refs):
    (images_h, targets_h, mask_h, ef_h, es_h, et_h, eo_h, df_h, ds_h, dt_h, do_h, *rest) = refs
    biases_h, rest = rest[:8], rest[8:]
    (decoded_h, images_grad_h, loss, tot0, tot1, tot2,
     images, targets, mask, ef_s, es_s, et_s, eo_s, df_s, ds_s, dt_s, do_s, *rest) = rest
    biases_s, rest = rest[:8], rest[8:]
    decoded, images_grad = images, targets
    (src, act0, sl_src, z1, z2, a3, y1, y2, y3, s1, s2, s3, t1, t2, t3,
     mid, sl_mid, d0, g4, h4, zg, zh, stage,
     w_ef, w_es, w_et, v_es, v_et, w_ds, w_dt, v_ds, v_dt, w_do, w_eo, w_df, bias, bacc, eacc,
     *rest) = rest
    whole, part, rest = rest[:3], rest[3:6], rest[6:]
    bufs0, bufs1, bufs2, rest = rest[:3], rest[3:12], rest[12:21], rest[21:]
    shard_sem, image_sem, io_sem, *pairs = rest

    nz = whole[0].shape[0]
    dp = nz * 2
    spots, widths = places(dp)
    me = where_am_i()
    z, y, x, c = me

    def near(src, dst, sem):
        cp = pltpu.make_async_copy(src, dst, sem)
        cp.start()
        return cp
    shards_h = (ef_h, es_h, et_h, eo_h, df_h, ds_h, dt_h, do_h, *biases_h)
    shards_s = (ef_s, es_s, et_s, eo_s, df_s, ds_s, dt_s, do_s, *biases_s)
    shard_copies = [near(p, q, shard_sem.at[k]) for k, (p, q) in enumerate(zip(shards_h, shards_s))]
    image_copies = [near(images_h.at[pl.ds(8 * k, 8)], images.at[pl.ds(8 * k, 8)], image_sem.at[k]) for k in range(4)]
    target_copy = near(targets_h, targets, io_sem.at[0])
    mask_copy = near(mask_h, mask, io_sem.at[1])

    barrier = pltpu.get_barrier_semaphore()
    others = [device(*other_chip(me, step, nz)) for step in chip_steps(nz)] + [device(z, y, x, 1 - c)]
    for d in others:
        pl.semaphore_signal(barrier, inc=1, device_id=d, device_id_type=MESH)
    g0 = DirectGather(me, whole[0], *pairs[0:2])
    g1 = Gather(me, whole[1], *pairs[2:4])
    g2 = Gather(me, whole[2], *pairs[4:6])
    wait_all(shard_copies)
    bias_part = bias_block([b[...].astype(F32) for b in biases_s]).astype(BF16)
    whole[0][z, y, x, c] = lanes_to([ef_s[...], es_s[...], bias_part], widths[0])
    pl.semaphore_wait(barrier, len(others))
    g0.chips()
    whole[1][z, y, x, c] = lanes_to([et_s[...], df_s[...], eo_block(eo_s[...].astype(F32)).astype(BF16)], widths[1])
    whole[2][z, y, x, c] = lanes_to([ds_s[...], dt_s[...]] + [do_s[16 * k:16 * k + 16] for k in range(4)], widths[2])
    g1.along_z()

    for ref in (act0, g4, z1, z2, y1, y2, y3, zg, zh):
        ref[0] = jnp.zeros(ref.shape[1:], ref.dtype)
        ref[33] = jnp.zeros(ref.shape[1:], ref.dtype)
    bacc[...] = jnp.zeros_like(bacc)
    eacc[...] = jnp.zeros_like(eacc)

    def blocks(name):
        g, at, n = spots[name]
        return [[whole[g][a // 2, a % 2, b // 2, b % 2, :, at:at + n] for b in range(4)] for a in range(dp)]

    def across(name):
        return jnp.concatenate([jnp.concatenate(col, axis=0) for col in blocks(name)], axis=1)

    def tap(k, i, n):
        return [k[:, (3 * i + j) * n:(3 * i + j + 1) * n] for j in range(3)]

    def quad_weights(k, w_ref, v_ref):
        w_ref[0, 128:256, :] = jnp.zeros((128, 256), BF16)
        w_ref[3, 0:128, :] = jnp.zeros((128, 256), BF16)
        v_ref[0, :, 128:256] = jnp.zeros((256, 128), BF16)
        v_ref[3, :, 0:128] = jnp.zeros((256, 128), BF16)
        for i in range(3):
            t = tap(k, i, 64)
            f = stack_out(t)
            w_ref[i, 0:128, :] = f
            w_ref[i + 1, 128:256, :] = f
            b = stack_in(t)
            v_ref[2 - i, :, 0:128] = b
            v_ref[3 - i, :, 128:256] = b

    def two(k):
        z = jnp.zeros_like(k)
        return jnp.concatenate([jnp.concatenate([k, z], axis=1), jnp.concatenate([z, k], axis=1)], axis=0)

    r_eo = 64 // dp

    def first_weights():
        k = across("ef")
        for i in range(3):
            w_ef[i] = stack_in(tap(k, i, 256))
        rows = [bias_rows(col[0].astype(F32), 64 // dp) for col in blocks("bias")]
        for n, k in enumerate((0, 1, 2, 4, 5, 6, 3, 7)):
            v = jnp.concatenate([r[k] for r in rows], axis=1)
            v = jnp.concatenate([v, v], axis=1)
            if n < 6:
                bias[n, :, 0:128] = v
            else:
                bias[n] = v * (1.0 / 64.0)
        quad_weights(across("es"), w_es, v_es)

    def second_weights():
        quad_weights(across("et"), w_et, v_et)
        w_eo[...] = two(jnp.concatenate([
            jnp.concatenate([blk.astype(F32)[0:r_eo] for blk in col], axis=1) for col in blocks("eo")], axis=0).astype(BF16))
        w_df[...] = two(across("df"))

    def third_weights():
        quad_weights(across("ds"), w_ds, v_ds)
        quad_weights(across("dt"), w_dt, v_dt)
        quarter = [across(k) for k in range(4)]
        k = jnp.concatenate([quarter[k][16 * b:16 * b + 16] for b in range(4) for k in range(4)], axis=0)
        for i in range(3):
            w_do[i] = stack_out(tap(k, i, 64))

    def to_pairs(v, slot):
        stage[slot, 0] = v[:, :128]
        stage[slot, 1] = v[:, 128:]
        return [jnp.concatenate([stage[slot, h, pl.ds(2 * t + e, 8, stride=16), :] for t in range(8)], axis=0)
                for e in range(2) for h in range(2)]

    def to_natural(v, slot):
        for e in range(2):
            for h in range(2):
                for t in range(8):
                    stage[slot, h, pl.ds(2 * t + e, 8, stride=16), :] = v[8 * t:8 * t + 8, e * 256 + h * 128:e * 256 + h * 128 + 128]
        return stage[slot, 0], stage[slot, 1]

    def source_rows(k):
        def body(r):
            p = 8 * k + r
            v = images[p].astype(F32)
            slot = p % 4 if isinstance(p, int) else lax.rem(p, 4)
            for q, x in enumerate(to_pairs(v, slot)):
                ln = slice(q * 128, q * 128 + 128)
                act, slope = silu_parts(x)
                src[p, :, ln] = x.astype(BF16)
                act0[p + 1, :, ln] = act.astype(BF16)
                sl_src[p, :, ln] = slope
        loop(8, body, U['B'])

    def hidden(pre, b, slope_ref, row):
        act, slope = silu_parts(pre + bias[b, :, 0:128])
        slope_ref[row] = slope
        return act

    def enc_first():
        n = U['nC']

        def body(c):
            p = c * n
            acc = 0.0
            for i in range(3):
                acc = acc + dot_t(act0[pl.ds(p + i, n)].reshape(n * 64, 512), w_ef[i])
            for r, a in enumerate(rows_of(acc, n)):
                put_pair(z1, p + r + 1, hidden(a[:, :128] + folded(a[None, :, 128:])[0], 0, s1, p + r))
        loop(32 // n, body, U['C'])

    def quad_conv(zin, w, b, slope_ref, zout, pair=True):
        n = U['nQ']

        def body(c):
            acc = 0.0
            for d in range(4):
                acc = acc + dot_t(quad_rows(zin, c * n, n, d), w[d])
            for r, a in enumerate(rows_of(acc, n)):
                for e in range(2):
                    row = (c * n + r) * 2 + e
                    act = hidden(a[:, 128 * e:128 * e + 128], b, slope_ref, row)
                    if pair:
                        put_pair(zout, row + 1, act)
                    else:
                        zout[row] = act.astype(BF16)
        loop(16 // n, body, U['Q'])

    def middle_rows():
        n = U['nF']

        def body(c):
            p = c * n
            br = dot(a3[pl.ds(p, n)].reshape(n * 64, 128), w_eo[...])
            for r, a in enumerate(rows_of(br, n)):
                for q in range(4):
                    ln = slice(128 * q, 128 * q + 128)
                    m = src[p + r, :, ln].astype(F32) + (a[:, ln] * (1.0 / 64.0) + bias[6, :, ln])
                    act, slope = silu_parts(m)
                    mid[p + r, :, ln] = m
                    sl_mid[p + r, :, ln] = slope
                    d0[p + r, :, ln] = act.astype(BF16)
            pre = dot_t(d0[pl.ds(p, n)].reshape(n * 64, 512), w_df[...])
            for r, a in enumerate(rows_of(pre, n)):
                put_pair(y1, p + r + 1, hidden(a, 3, t1, p + r))
        loop(32 // n, body, U['F'])

    def result_rows():
        mk = mask[...].astype(F32)
        tall = jnp.sum(mk[:, 0:1])
        broad = jnp.sum(mk[0:1, :])
        sub = lax.broadcasted_iota(jnp.int32, (64, 128), 0)
        column = lax.rem(sub, 8) * 16 + 2 * (sub // 8)
        wi = broad.astype(jnp.int32)
        hi = tall.astype(jnp.int32)
        col_mask = [jnp.where(column + e < wi, 1.0, 0.0) for e in range(2)]
        n = U['nJ']

        def body(c):
            p = c * n
            acc = 0.0
            for i in range(3):
                acc = acc + dot_t(y3[pl.ds(p + i, n)].reshape(n * 64, 256), w_do[i])
            acc = acc.reshape(n, 64, 512)
            for r in range(n):
                m = mid[p + r]
                res = m + (acc[r] * (1.0 / 64.0) + bias[7])
                src[p + r] = res.astype(BF16)
                t = to_pairs(targets[p + r].astype(F32), r % 4)
                row_on = jnp.where(p + r < hi, 1.0, 0.0)
                for q in range(4):
                    ln = slice(q * 128, q * 128 + 128)
                    diff = res[:, ln] - t[q]
                    g = diff * (col_mask[q // 2] * row_on)
                    mid[p + r, :, ln] = g
                    eacc[...] += part_sum(g * diff)
                    g = g * (1.0 / 64.0)
                    g4[p + r + 1, :, ln] = g.astype(BF16)
                    bacc[7, :, ln] += part_sum(g)
        loop(32 // n, body, U['J'])
        return tall * broad

    def decoded_rows(k):
        def body(r):
            p = 8 * k + r
            a, b = to_natural(src[p].astype(F32), p % 4 if isinstance(p, int) else lax.rem(p, 4))
            decoded[p, :, 0:128] = a.astype(BF16)
            decoded[p, :, 128:256] = b.astype(BF16)
        loop(8, body, U['B'])
        return near(decoded.at[pl.ds(8 * k, 8)], decoded_h.at[pl.ds(8 * k, 8)], io_sem.at[2 + k])

    def back(x, slope_ref, row, b):
        g = x * slope_ref[row]
        bacc[b, :, 0:128] += part_sum(g)
        return g

    def dec_last_back():
        n = U['nC']

        def body(c):
            p = c * n
            acc = 0.0
            for i in range(3):
                acc = acc + dot(g4[pl.ds(p + i, n)].reshape(n * 64, 512), w_do[2 - i])
            for r, a in enumerate(rows_of(acc, n)):
                put_pair(zg, p + r + 1, back(a[:, :128] + folded(a[None, :, 128:])[0], t3, p + r, 5))
        loop(32 // n, body, U['K'])

    M = [3, 0, 1, 2]

    def dec_last_weights():
        gv = g4[pl.ds(1, 32)].reshape(2048, 512)
        cols = []
        for i in range(3):
            t = dot_p(gv, y3[pl.ds(i, 32)].reshape(2048, 256))
            for j in range(3):
                a, b = M[j] * 64, M[j + 1] * 64
                cols.append(t[0:256, a:a + 64] + t[256:512, b:b + 64])
        k_do = jnp.concatenate(cols, axis=1).astype(BF16)
        for a in range(dp):
            n = 576 // dp
            v = k_do[:, n * a:n * a + n]
            for b in range(4):
                for k in range(4):
                    at = spots[k][1]
                    r = 64 * b + 16 * k
                    part[2][a // 2, a % 2, b // 2, b % 2, :, at:at + n] = v[r:r + 16]

    def deal(name, k):
        g, at, n = spots[name]
        k = k.astype(BF16)
        for a in range(dp):
            v = k[:, n * a:n * a + n]
            for b in range(4):
                part[g][a // 2, a % 2, b // 2, b % 2, :, at:at + n] = v[16 * b:16 * b + 16]

    def quad_wgrad(z, g_ref, name):
        gq = jnp.concatenate([
            jnp.concatenate([g_ref[2 * r + 1, :, 0:128] for r in range(16)], axis=0),
            jnp.concatenate([g_ref[2 * r + 2, :, 0:128] for r in range(16)], axis=0)], axis=1)
        t = [dot_p(gq, quad_rows(z, 0, 16, d)) for d in range(4)]
        cols = []
        for i in range(3):
            s = t[i][0:128] + t[i + 1][128:256]
            for j in range(3):
                a, b = M[j] * 64, M[j + 1] * 64
                cols.append(s[0:64, a:a + 64] + s[64:128, b:b + 64])
        deal(name, jnp.concatenate(cols, axis=1))

    def quad_back(zin, v, slope_ref, b, zout):
        n = U['nQ']

        def body(c):
            acc = 0.0
            for d in range(4):
                acc = acc + dot(quad_rows(zin, c * n, n, d), v[d])
            for r, a in enumerate(rows_of(acc, n)):
                for e in range(2):
                    row = (c * n + r) * 2 + e
                    put_pair(zout, row + 1, back(a[:, 128 * e:128 * e + 128], slope_ref, row, b))
        loop(16 // n, body, U['Q'])

    def dec_first_weights():
        t = dot_p(zg[pl.ds(1, 32), :, 0:128].reshape(2048, 128), d0[...].reshape(2048, 512))
        deal("df", t[0:64, 0:256] + t[64:128, 256:512])

    def middle_back():
        n = U['nF']

        def body(c):
            p = c * n
            bk = dot(zg[pl.ds(p + 1, n), :, 0:128].reshape(n * 64, 128), w_df[...])
            for r, a in enumerate(rows_of(bk, n)):
                for q in range(4):
                    ln = slice(128 * q, 128 * q + 128)
                    gm = mid[p + r, :, ln] + sl_mid[p + r, :, ln] * a[:, ln]
                    mid[p + r, :, ln] = gm
                    g = gm * (1.0 / 64.0)
                    bacc[6, :, ln] += part_sum(g)
                    h4[p + r, :, ln] = g.astype(BF16)
            x = dot_t(h4[pl.ds(p, n)].reshape(n * 64, 512), w_eo[...])
            for r, a in enumerate(rows_of(x, n)):
                put_pair(zh, p + r + 1, back(a, s3, p + r, 2))
        loop(32 // n, body, U['F'])

    def enc_last_weights():
        t = dot_p(a3[...].reshape(2048, 128), h4[...].reshape(2048, 512))
        k = t[0:64, 0:256] + t[64:128, 256:512]
        g, at, n = spots["eo"]
        for a in range(dp):
            for b in range(4):
                v = eo_block(k[a * r_eo:a * r_eo + r_eo, 64 * b:64 * b + 64])
                part[g][a // 2, a % 2, b // 2, b % 2, :, at:at + n] = v.astype(BF16)

    def enc_first_weights():
        gv = zh[pl.ds(1, 32)].reshape(2048, 256)
        cols = []
        for i in range(3):
            t = dot_p(gv, act0[pl.ds(i, 32)].reshape(2048, 512))
            cols.append(t[64:128, 0:256] + t[128:192, 256:512])
            cols.append(t[0:64, 0:256] + t[64:128, 256:512])
            cols.append(t[192:256, 0:256] + t[0:64, 256:512])
        deal("ef", jnp.concatenate(cols, axis=1))

    def deal_biases():
        sums = []
        for n in (0, 1, 2, 6, 3, 4, 5, 7):
            v = jnp.sum(bacc[n], axis=0, keepdims=True)
            sums.append(v[:, 0:256] + v[:, 256:512] if n >= 6 else v[:, 0:64] + v[:, 64:128])
        g, at, n = spots["bias"]
        for a in range(dp):
            v = bias_block([q[:, a * (q.shape[1] // dp):(a + 1) * (q.shape[1] // dp)] for q in sums]).astype(BF16)
            for b in range(4):
                part[g][a // 2, a % 2, b // 2, b % 2, :, at:at + n] = v

    def source_grad(k):
        n = U['nG']

        def body(c):
            p = 8 * k + c * n
            acc = 0.0
            for i in range(3):
                acc = acc + dot(zh[pl.ds(p + i, n)].reshape(n * 64, 256), w_ef[2 - i])
            acc = acc.reshape(n, 64, 512)
            for r in range(n):
                g = mid[p + r] + sl_src[p + r] * acc[r]
                a, b = to_natural(g, r % 4)
                images_grad[p + r, :, 0:128] = a.astype(BF16)
                images_grad[p + r, :, 128:256] = b.astype(BF16)
        loop(8 // n, body, U['Qr'])

    def source_grad_out(k):
        return near(images_grad.at[pl.ds(8 * k, 8)], images_grad_h.at[pl.ds(8 * k, 8)], image_sem.at[k])

    run = lambda name, f, *args: f(*args)
    for k in range(4):
        image_copies[k].wait()
        run('src%d' % k, source_rows, k)
    g1.square_one()
    g0.cores()
    g2.along_z()
    g0.finish()
    g1.square_two()
    run('w0', first_weights)
    run('enc1', enc_first)
    g1.cores()
    g2.square_one()
    run('enc2', quad_conv, z1, w_es, 1, s2, z2)
    g1.finish()
    run('w1', second_weights)
    g2.square_two()
    run('enc3', quad_conv, z2, w_et, 2, s3, a3, False)
    g2.cores()
    run('middle', middle_rows)
    g2.finish()
    run('w2', third_weights)
    run('dec2', quad_conv, y1, w_ds, 4, t2, y2)
    run('dec3', quad_conv, y2, w_dt, 5, t3, y3)
    mask_copy.wait()
    target_copy.wait()
    pixels = run('result', result_rows)
    loss[0] = 0.5 * jnp.sum(eacc[...]) / (pixels * 256.0)
    run('dec4b', dec_last_back)
    run('dec4w', dec_last_weights)
    run('dec3b', quad_back, zg, v_dt, t2, 4, zh)
    run('dec3w', quad_wgrad, y2, zg, "dt")
    run('dec2b', quad_back, zh, v_ds, t1, 3, zg)
    run('dec2w', quad_wgrad, y1, zh, "ds")
    r2 = Scatter(me, part[2], bufs2, *pairs[6:8])
    r2.cores()
    run('dec1w', dec_first_weights)
    run('midb', middle_back)
    r2.square_one()
    run('enc4w', enc_last_weights)
    run('enc3w', quad_wgrad, z2, zh, "et")
    r1 = Scatter(me, part[1], bufs1, *pairs[8:10])
    r1.cores()
    run('enc3b', quad_back, zh, v_et, s2, 1, zg)
    r2.square_two()
    run('enc2w', quad_wgrad, z1, zg, "es")
    run('enc2b', quad_back, zg, v_es, s1, 0, zh)
    run('bias', deal_biases)
    r1.square_one()
    run('enc1w', enc_first_weights)
    r0 = DirectScatter(me, part[0], bufs0, *pairs[10:12])
    r0.cores()
    r2.along_z()
    out_copies = []
    for k in range(2):
        out_copies.append(run('out%d' % k, decoded_rows, k))
    r1.square_two()
    run('grad0', source_grad, 0)
    out_copies.append(source_grad_out(0))
    r0.chips()
    for k in range(1, 4):
        run('grad%d' % k, source_grad, k)
        out_copies.append(source_grad_out(k))
    r1.along_z()
    for k in range(2, 4):
        out_copies.append(run('out%d' % k, decoded_rows, k))
    r2.finish(tot2)
    r1.finish(tot1)
    r0.finish(tot0)
    wait_all(out_copies)


def last_kernel(decoded_i, images_grad_i, loss_i, *refs):
    tots_i, (decoded, images_grad, loss), refs = refs[:3], refs[3:6], refs[6:]
    outs_h, refs = refs[:16], refs[16:]
    outs, tots, hold, sem, tot_sem, out_sem = refs[:16], refs[16:19], *refs[19:]
    dp = 64 // outs[3].shape[0]
    small = [pltpu.make_async_copy(p, q, tot_sem.at[k]) for k, (p, q) in enumerate(zip(tots_i, tots))]
    pairs = [(p, q, n * 4 + k, pl.ds(8 * k, 8)) for k in range(4) for n, (p, q) in enumerate(((decoded_i, decoded), (images_grad_i, images_grad)))]
    ins = [pltpu.make_async_copy(p.at[rows], hold.at[k], sem.at[k]) for p, q, k, rows in pairs]
    backs = [pltpu.make_async_copy(hold.at[k], q.at[rows], sem.at[8 + k]) for p, q, k, rows in pairs]
    for cp in small + ins:
        cp.start()
    loss[0] = loss_i[0]
    wait_all(small)
    spots, _ = places(dp)

    def piece(name):
        g, at, n = spots[name]
        return tots[g][:, at:at + n]
    for k, name in enumerate(("ef", "es", "et", None, "df", "ds", "dt")):
        if name:
            outs[k][...] = piece(name)
    outs[3][...] = piece("eo")[0:64 // dp]
    for k in range(4):
        outs[7][16 * k:16 * k + 16] = piece(k)
    for ref, v in zip(outs[8:], bias_rows(piece("bias"), 64 // dp)):
        ref[...] = v
    last = [pltpu.make_async_copy(p, q, out_sem.at[k]) for k, (p, q) in enumerate(zip(outs, outs_h))]
    for cp in last:
        cp.start()
    for p, q in zip(ins, backs):
        p.wait()
        q.start()
    wait_all(last + backs)


U = dict(B=4, nC=32, C=1, K=1, nQ=16, Q=1, nF=16, F=1, nJ=16, J=1, nG=8, Qr=1)


def per_device(images, targets, pixel_mask, ef, es, et, eo, eba, ebb, ebc, ebd, df, ds, dt, do, dba, dbb, dbc, dbd):
    dp = lax.axis_size("dp")
    nz = dp // 2
    h = nz // 2
    widths = places(dp)[1]
    chips = len(chip_steps(nz))
    vm = pl.BlockSpec(memory_space=pltpu.VMEM)
    far = pl.BlockSpec(memory_space=pl.ANY)
    smem = pl.BlockSpec(memory_space=pltpu.SMEM)
    sem = pltpu.SemaphoreType.DMA
    V = lambda shape, dt: pltpu.VMEM(shape, dt)
    S = jax.ShapeDtypeStruct
    args = [images[0], targets[0], pixel_mask[0], ef.T, es.T, et.T, eo, df.T, ds.T, dt.T, do.T]
    args += [b.reshape(1, -1) for b in (eba, ebb, ebc, ebd, dba, dbb, dbc, dbd)]
    comm = lambda wide: [
        V((nz, 2, 2, 16, wide), BF16), V((nz, 2, 2, 16, wide), BF16), V((h, 2, 16, wide), BF16), V((nz - h, 2, 16, wide), BF16),
        V((h, 2, 16, wide), BF16), V((nz - h, 2, 16, wide), BF16), V((nz, 16, wide), BF16), V((nz, 16, wide), BF16),
        V((nz, 16, wide), BF16)]
    direct = [V((nz, 2, 2, 16, widths[0]), BF16)] * 2 + [V((chips, 16, widths[0]), BF16)]
    big = S((32, 128, 256), BF16)
    tots = [S((16, w), F32) for w in widths]
    decoded, images_grad, loss, *kept = pl.pallas_call(
        functools.partial(main_kernel, U),
        out_shape=[big, big, S((1,), F32), *tots],
        in_specs=[far] * 19, out_specs=[far, far, smem, vm, vm, vm],
        scratch_shapes=[V(a.shape, a.dtype) for a in args] + [
            V((32, 64, 512), BF16), V((34, 64, 512), BF16), V((32, 64, 512), F32),
            V((34, 64, 256), BF16), V((34, 64, 256), BF16), V((32, 64, 128), BF16),
            V((34, 64, 256), BF16), V((34, 64, 256), BF16), V((34, 64, 256), BF16)] + [V((32, 64, 128), F32)] * 6 + [
            V((32, 64, 512), F32), V((32, 64, 512), F32), V((32, 64, 512), BF16),
            V((34, 64, 512), BF16), V((32, 64, 512), BF16), V((34, 64, 256), BF16), V((34, 64, 256), BF16),
            V((4, 2, 128, 128), F32),
            V((3, 256, 512), BF16)] + [V((4, 256, 256), BF16)] * 8 + [
            V((3, 512, 256), BF16), V((128, 512), BF16), V((128, 512), BF16),
            V((8, 1, 512), F32), V((8, 8, 512), F32), V((8, 128), F32)]
        + [V((nz, 2, 2, 2, 16, w), BF16) for w in widths] * 2 + direct + comm(widths[1]) + comm(widths[2])
        + [sem((16,)), sem((4,)), sem((6,))] + [sem((chips + nz,))] * 2 + [sem((nz + 4,))] * 8 + [sem((chips + 1,))] * 2,
        compiler_params=pltpu.CompilerParams(collective_id=0, has_side_effects=True, vmem_limit_bytes=63 * 2**20),
    )(*args)
    f = lambda *s: S(s, F32)
    grads = [f(16, 2304 // dp), f(16, 576 // dp), f(16, 576 // dp), f(64 // dp, 64), f(16, 256 // dp),
             f(16, 576 // dp), f(16, 576 // dp), f(64, 576 // dp)] + [f(1, s // dp) for s in (64, 64, 64, 256) * 2]
    outs = pl.pallas_call(
        last_kernel,
        out_shape=[big, big, S((1,), F32)] + grads,
        in_specs=[far, far, smem, far, far, far], out_specs=[far, far, smem] + [far] * 16,
        scratch_shapes=[V(g.shape, F32) for g in grads + tots] + [V((8, 8, 128, 256), BF16), sem((16,)), sem((3,)), sem((16,))],
        compiler_params=pltpu.CompilerParams(vmem_limit_bytes=60 * 2**20),
    )(decoded, images_grad, loss, *kept)
    decoded, images_grad, loss, g_ef, g_es, g_et, g_eo, g_df, g_ds, g_dt, g_do = outs[:11]
    bs = [b.reshape(-1) for b in outs[11:]]
    return (decoded[None], images_grad[None], loss, g_ef.T, g_es.T, g_et.T, g_eo, *bs[:4],
            g_df.T, g_ds.T, g_dt.T, g_do.T, *bs[4:])


def solution(mesh):
    img, w, b = P(("dp", "fsdp"), None, None, None), P("dp", "fsdp"), P("dp")
    placed = (img, img, P(("dp", "fsdp"), None, None)) + (w,) * 4 + (b,) * 4 + (w,) * 4 + (b,) * 4
    return jax.shard_map(
        per_device, mesh=mesh, in_specs=placed,
        out_specs=(img, img, P(("dp", "fsdp"))) + (w,) * 4 + (b,) * 4 + (w,) * 4 + (b,) * 4,
        check_vma=False)
```

```python
import functools
import jax
import jax.numpy as jnp
from jax import lax
from jax.experimental import pallas as pl
from jax.experimental.pallas import tpu as pltpu
from jax.sharding import PartitionSpec as P

F32, BF16 = jnp.float32, jnp.bfloat16
MESH = pl.DeviceIdType.MESH


def dot(a, b):
    return jnp.dot(a, b, preferred_element_type=F32)


def dot_t(a, b):
    return lax.dot_general(a, b, (((1,), (1,)), ((), ())), preferred_element_type=F32)


def dot_p(a, b):
    return lax.dot_general(a, b, (((0,), (0,)), ((), ())), preferred_element_type=F32)


def loop(count, body, unroll):
    if unroll >= count:
        for c in range(count):
            body(c)
    else:
        def step(k, _):
            for u in range(unroll):
                body(k * unroll + u)
            return 0
        lax.fori_loop(0, count // unroll, step, 0)


def masks():
    lane = lax.broadcasted_iota(jnp.int32, (1, 1, 8, 128), 3)
    row = lax.broadcasted_iota(jnp.int32, (1, 1, 8, 128), 2)
    return lane < 64, row


def shifted(x):
    n = x.shape[0]
    _, row = masks()
    x4 = x.reshape(n, 8, 8, 128)
    nxt = jnp.where(row == 7, 0.0, pltpu.roll(x4[:, :1], 7, 2))
    prv = jnp.where(row == 0, 0.0, pltpu.roll(x4[:, 7:], 1, 2))
    up = jnp.concatenate([x4[:, 1:], nxt], axis=1)
    dn = jnp.concatenate([prv, x4[:, :7]], axis=1)
    return up, dn


def beside(x):
    lo, _ = masks()
    up, dn = shifted(x)
    return jnp.where(lo, up, dn).reshape(x.shape)


def folded(x):
    lo, _ = masks()
    up, dn = shifted(x)
    return jnp.where(lo, dn, up).reshape(x.shape)


def silu_parts(v):
    h = 0.5 * v
    u = 1.0 + jnp.tanh(h)
    act = h * u
    w = 0.5 * u
    return act, w + act * (1.0 - w)


def part_sum(x):
    return x.reshape(-1, 8, x.shape[-1]).sum(axis=0)


def put_pair(ref, idx, x):
    ref[idx, :, 0:128] = x.astype(BF16)
    ref[idx, :, 128:256] = beside(x[None])[0].astype(BF16)


def quad_rows(ref, r0, n, d):
    return jnp.concatenate([ref[2 * (r0 + k) + d] for k in range(n)], axis=0)


def rows_of(x, n):
    return [x[64 * r:64 * r + 64] for r in range(n)]


def stack_in(k):
    z = jnp.zeros_like(k[0])
    rows = ((k[1], k[2]), (k[0], k[1]), (z, k[0]), (k[2], z))
    return jnp.concatenate([jnp.concatenate(r, axis=1) for r in rows], axis=0)


def stack_out(k):
    z = jnp.zeros_like(k[0])
    rows = ((k[1], k[2], z, k[0]), (k[0], k[1], k[2], z))
    return jnp.concatenate([jnp.concatenate(r, axis=1) for r in rows], axis=0)


TAPS = ("ef", "es", "et", "df", "ds", "dt")
ROWS = dict(ef=2304, es=576, et=576, df=256, ds=576, dt=576, do=576)


def places(dp):
    groups = ((("ef", 2304 // dp), ("es", 576 // dp), ("bias", 128 // dp)),
              (("et", 576 // dp), ("df", 256 // dp), ("eo", 64)),
              (("ds", 576 // dp), ("dt", 576 // dp)) + tuple((k, 576 // dp) for k in range(4)))
    spots, widths = {}, []
    for g, group in enumerate(groups):
        at = 0
        for name, n in group:
            spots[name] = (g, at, n)
            at += n
        widths.append(at + (-at % 128))
    return spots, widths


def bias_block(parts):
    w = parts[3].shape[1] // 2
    n = parts[0].shape[1]
    fill = lambda v: jnp.concatenate([v, jnp.zeros((1, w - n), F32)], axis=1)
    rows = [fill(parts[k]) for k in (0, 1, 2, 4, 5, 6)]
    for k in (3, 7):
        rows += [parts[k][:, :w], parts[k][:, w:]]
    return jnp.concatenate(rows + [jnp.zeros((6, w), F32)], axis=0)


def bias_rows(block, n):
    thin = [block[k:k + 1, :n] for k in range(6)]
    wide = [jnp.concatenate([block[k:k + 1], block[k + 1:k + 2]], axis=1) for k in (6, 8)]
    return thin[:3] + wide[:1] + thin[3:] + wide[1:]


def eo_block(eo):
    return jnp.concatenate([eo, jnp.zeros((16 - eo.shape[0], 64), F32)], axis=0)


def lanes_to(parts, wide):
    at = sum(p.shape[1] for p in parts)
    if at < wide:
        parts = parts + [jnp.zeros((parts[0].shape[0], wide - at), parts[0].dtype)]
    return jnp.concatenate(parts, axis=1)


def where_am_i():
    a, b = lax.axis_index("dp"), lax.axis_index("fsdp")
    return a // 2, lax.rem(a, 2), b // 2, lax.rem(b, 2)


def device(z, y, x, c):
    return (z * 2 + y, x * 2 + c)


def far_copy(src, dst, send, recv, to):
    cp = pltpu.make_async_remote_copy(
        src_ref=src, dst_ref=dst, send_sem=send, recv_sem=recv, device_id=to, device_id_type=MESH)
    cp.start()
    return cp


def wait_all(copies):
    for cp in copies:
        cp.wait()


class Gather:
    def __init__(self, me, buf, send, recv):
        self.me, self.buf, self.send, self.recv = me, buf, send, recv
        self.nz = buf.shape[0]
        self.h = self.nz // 2

    def copy(self, view, k, to):
        return far_copy(view, view, self.send.at[k], self.recv.at[k], device(*to))

    def along_z(self):
        z, y, x, c = self.me
        mine = self.buf.at[z, y, x, c]
        self.fly = [self.copy(mine, 3 + k, (lax.rem(z + k, self.nz), y, x, c)) for k in range(1, self.nz)]

    def square_one(self):
        z, y, x, c = self.me
        wait_all(self.fly)
        lo, hi = pl.ds(0, self.h), pl.ds(self.h, self.nz - self.h)
        self.fly = [self.copy(self.buf.at[lo, y, x, c], 0, (z, 1 - y, x, c)),
                    self.copy(self.buf.at[hi, y, x, c], 1, (z, y, 1 - x, c))]

    def square_two(self):
        z, y, x, c = self.me
        wait_all(self.fly)
        lo, hi = pl.ds(0, self.h), pl.ds(self.h, self.nz - self.h)
        self.fly = [self.copy(self.buf.at[lo, :, x, c], 2, (z, y, 1 - x, c)),
                    self.copy(self.buf.at[hi, y, :, c], 3, (z, 1 - y, x, c))]

    def cores(self):
        z, y, x, c = self.me
        wait_all(self.fly)
        self.fly = [self.copy(self.buf.at[:, :, :, c], self.nz + 3, (z, y, x, 1 - c))]

    def finish(self):
        wait_all(self.fly)


class DirectGather:
    def __init__(self, me, buf, send, recv):
        self.me, self.buf, self.send, self.recv = me, buf, send, recv
        self.nz = buf.shape[0]
        self.steps = chip_steps(self.nz)

    def copy(self, view, k, to):
        return far_copy(view, view, self.send.at[k], self.recv.at[k], device(*to))

    def chips(self):
        z, y, x, c = self.me
        mine = self.buf.at[z, y, x, c]
        self.fly = {}
        for k, step in reversed(list(enumerate(self.steps))):
            self.fly[k] = self.copy(mine, k, other_chip(self.me, step, self.nz))

    def cores(self):
        z, y, x, c = self.me
        self.last = []
        for dz in range(self.nz):
            wait_all([self.fly[k] for k, step in enumerate(self.steps) if step[0] == dz])
            rows = self.buf.at[lax.rem(z + self.nz - dz, self.nz), :, :, c]
            self.last.append(self.copy(rows, len(self.steps) + dz, (z, y, x, 1 - c)))

    def finish(self):
        wait_all(self.last)


class DirectScatter:
    def __init__(self, me, part, bufs, send, recv):
        self.me, self.part, self.send, self.recv = me, part, send, recv
        self.in1, self.s1, self.in2 = bufs
        self.nz = part.shape[0]
        self.steps = chip_steps(self.nz)
        self.fly = []

    def copy(self, src, dst, k, to):
        return far_copy(src, dst, self.send.at[k], self.recv.at[k], device(*to))

    def cores(self, k, lo, hi):
        z, y, x, c = self.me
        rows = pl.ds(lo, hi - lo)
        self.fly.append(self.copy(self.part.at[rows, :, :, 1 - c], self.in1.at[rows], len(self.steps) + k, (z, y, x, 1 - c)))

    def chips(self):
        z, y, x, c = self.me
        wait_all(self.fly)
        for k in range(self.nz):
            self.s1[k] = add16(self.part[k, :, :, c], self.in1[k])
        self.fly = []
        for k, step in reversed(list(enumerate(self.steps))):
            to = other_chip(self.me, step, self.nz)
            self.fly.append(self.copy(self.s1.at[to[0], to[1], to[2]], self.in2.at[k], k, to))

    def finish(self, out):
        z, y, x, c = self.me
        wait_all(self.fly)
        total = self.s1[z, y, x].astype(F32)
        for k in range(len(self.steps)):
            total = total + self.in2[k].astype(F32)
        out[...] = total


def chip_steps(nz):
    return [(dz, dy, dx) for dz in range(nz) for dy in range(2) for dx in range(2)][1:]


def other_chip(me, step, nz):
    z, y, x, c = me
    return (lax.rem(z + step[0], nz), lax.rem(y + step[1], 2), lax.rem(x + step[2], 2), c)


def add16(p, q):
    return (p.astype(F32) + q.astype(F32)).astype(BF16)


def main_kernel(U, *refs):
    (images_h, targets_h, mask_h, ef_h, es_h, et_h, eo_h, df_h, ds_h, dt_h, do_h, *rest) = refs
    biases_h, rest = rest[:8], rest[8:]
    (decoded_h, images_grad_h, loss, tot0, tot1, tot2,
     images, targets, mask, ef_s, es_s, et_s, eo_s, df_s, ds_s, dt_s, do_s, *rest) = rest
    biases_s, rest = rest[:8], rest[8:]
    decoded, images_grad = images, targets
    (src, act0, sl_src, z1, z2, a3, y1, y2, y3, s1, s2, s3, t1, t2, t3,
     mid, sl_mid, d0, g4, h4, zg, zh, stage,
     w_ef, w_es, w_et, v_es, v_et, w_ds, w_dt, v_ds, v_dt, w_do, w_eo, w_df, bias, bacc, eacc, tp,
     *rest) = rest
    whole, part, rest = rest[:3], rest[3:6], rest[6:]
    bufs0, bufs1, bufs2, rest = rest[:3], rest[3:6], rest[6:9], rest[9:]
    shard_sem, image_sem, io_sem, *pairs = rest

    nz = whole[0].shape[0]
    dp = nz * 2
    spots, widths = places(dp)
    me = where_am_i()
    z, y, x, c = me

    barrier = pltpu.get_barrier_semaphore()
    others = [device(*other_chip(me, step, nz)) for step in chip_steps(nz)] + [device(z, y, x, 1 - c)]
    for d in others:
        pl.semaphore_signal(barrier, inc=1, device_id=d, device_id_type=MESH)

    def near(src, dst, sem):
        cp = pltpu.make_async_copy(src, dst, sem)
        cp.start()
        return cp
    shards_h = (ef_h, es_h, et_h, eo_h, df_h, ds_h, dt_h, do_h, *biases_h)
    shards_s = (ef_s, es_s, et_s, eo_s, df_s, ds_s, dt_s, do_s, *biases_s)
    shard_copies = [near(p, q, shard_sem.at[k]) for k, (p, q) in enumerate(zip(shards_h, shards_s))]
    image_copies = [near(images_h.at[pl.ds(8 * k, 8)], images.at[pl.ds(8 * k, 8)], image_sem.at[k]) for k in range(4)]
    target_copy = near(targets_h, targets, io_sem.at[0])
    mask_copy = near(mask_h, mask, io_sem.at[1])

    g0 = DirectGather(me, whole[0], *pairs[0:2])
    g1 = Gather(me, whole[1], *pairs[2:4])
    g2 = DirectGather(me, whole[2], *pairs[4:6])
    wait_all(shard_copies)
    bias_part = bias_block([b[...].astype(F32) for b in biases_s]).astype(BF16)
    whole[0][z, y, x, c] = lanes_to([ef_s[...], es_s[...], bias_part], widths[0])
    pl.semaphore_wait(barrier, len(others))
    g0.chips()
    whole[1][z, y, x, c] = lanes_to([et_s[...], df_s[...], eo_block(eo_s[...].astype(F32)).astype(BF16)], widths[1])
    whole[2][z, y, x, c] = lanes_to([ds_s[...], dt_s[...]] + [do_s[16 * k:16 * k + 16] for k in range(4)], widths[2])
    g1.along_z()

    for ref in (act0, g4, z1, z2, y1, y2, y3, zg, zh):
        ref[0] = jnp.zeros(ref.shape[1:], ref.dtype)
        ref[33] = jnp.zeros(ref.shape[1:], ref.dtype)
    bacc[...] = jnp.zeros_like(bacc)
    eacc[...] = jnp.zeros_like(eacc)

    def blocks(name):
        g, at, n = spots[name]
        return [[whole[g][a // 2, a % 2, b // 2, b % 2, :, at:at + n] for b in range(4)] for a in range(dp)]

    def across(name):
        return jnp.concatenate([jnp.concatenate(col, axis=0) for col in blocks(name)], axis=1)

    def tap(k, i, n):
        return [k[:, (3 * i + j) * n:(3 * i + j + 1) * n] for j in range(3)]

    def quad_weights(k, w_ref, v_ref):
        w_ref[0, 128:256, :] = jnp.zeros((128, 256), BF16)
        w_ref[3, 0:128, :] = jnp.zeros((128, 256), BF16)
        v_ref[0, :, 128:256] = jnp.zeros((256, 128), BF16)
        v_ref[3, :, 0:128] = jnp.zeros((256, 128), BF16)
        for i in range(3):
            t = tap(k, i, 64)
            f = stack_out(t)
            w_ref[i, 0:128, :] = f
            w_ref[i + 1, 128:256, :] = f
            b = stack_in(t)
            v_ref[2 - i, :, 0:128] = b
            v_ref[3 - i, :, 128:256] = b

    def two(k):
        z = jnp.zeros_like(k)
        return jnp.concatenate([jnp.concatenate([k, z], axis=1), jnp.concatenate([z, k], axis=1)], axis=0)

    r_eo = 64 // dp

    def first_weights():
        k = across("ef")
        for i in range(3):
            w_ef[i] = stack_in(tap(k, i, 256))
        rows = [bias_rows(col[0].astype(F32), 64 // dp) for col in blocks("bias")]
        for n, k in enumerate((0, 1, 2, 4, 5, 6, 3, 7)):
            v = jnp.concatenate([r[k] for r in rows], axis=1)
            v = jnp.concatenate([v, v], axis=1)
            if n < 6:
                bias[n, :, 0:128] = v
            else:
                bias[n] = v * (1.0 / 64.0)
        quad_weights(across("es"), w_es, v_es)

    def second_weights():
        quad_weights(across("et"), w_et, v_et)
        w_eo[...] = two(jnp.concatenate([
            jnp.concatenate([blk.astype(F32)[0:r_eo] for blk in col], axis=1) for col in blocks("eo")], axis=0).astype(BF16))
        w_df[...] = two(across("df"))

    def third_weights():
        quad_weights(across("ds"), w_ds, v_ds)
        quad_weights(across("dt"), w_dt, v_dt)
        quarter = [across(k) for k in range(4)]
        k = jnp.concatenate([quarter[k][16 * b:16 * b + 16] for b in range(4) for k in range(4)], axis=0)
        for i in range(3):
            w_do[i] = stack_out(tap(k, i, 64))

    def to_pairs(v, slot):
        stage[slot, 0] = v[:, :128]
        stage[slot, 1] = v[:, 128:]
        return [jnp.concatenate([stage[slot, h, pl.ds(2 * t + e, 8, stride=16), :] for t in range(8)], axis=0)
                for e in range(2) for h in range(2)]

    def to_natural(v, slot):
        for e in range(2):
            for h in range(2):
                for t in range(8):
                    stage[slot, h, pl.ds(2 * t + e, 8, stride=16), :] = v[8 * t:8 * t + 8, e * 256 + h * 128:e * 256 + h * 128 + 128]
        return stage[slot, 0], stage[slot, 1]

    def source_rows(k):
        def body(r):
            p = 8 * k + r
            v = images[p].astype(F32)
            slot = p % 4 if isinstance(p, int) else lax.rem(p, 4)
            for q, x in enumerate(to_pairs(v, slot)):
                ln = slice(q * 128, q * 128 + 128)
                act, slope = silu_parts(x)
                src[p, :, ln] = x.astype(BF16)
                act0[p + 1, :, ln] = act.astype(BF16)
                sl_src[p, :, ln] = slope
        loop(8, body, U['B'])

    def target_rows():
        def body(p):
            slot = p % 4 if isinstance(p, int) else lax.rem(p, 4)
            for q, t in enumerate(to_pairs(targets[p].astype(F32), slot)):
                tp[p, :, q * 128:q * 128 + 128] = t.astype(BF16)
        loop(32, body, U['B'])

    def hidden(pre, b, slope_ref, row):
        act, slope = silu_parts(pre + bias[b, :, 0:128])
        slope_ref[row] = slope
        return act

    def enc_first():
        n = U['nC']

        def body(c):
            p = c * n
            acc = 0.0
            for i in range(3):
                acc = acc + dot_t(act0[pl.ds(p + i, n)].reshape(n * 64, 512), w_ef[i])
            for r, a in enumerate(rows_of(acc, n)):
                put_pair(z1, p + r + 1, hidden(a[:, :128] + folded(a[None, :, 128:])[0], 0, s1, p + r))
        loop(32 // n, body, U['C'])

    def quad_conv(zin, w, b, slope_ref, zout, pair=True):
        n = U['nQ']

        def body(c):
            acc = 0.0
            for d in range(4):
                acc = acc + dot_t(quad_rows(zin, c * n, n, d), w[d])
            for r, a in enumerate(rows_of(acc, n)):
                for e in range(2):
                    row = (c * n + r) * 2 + e
                    act = hidden(a[:, 128 * e:128 * e + 128], b, slope_ref, row)
                    if pair:
                        put_pair(zout, row + 1, act)
                    else:
                        zout[row] = act.astype(BF16)
        loop(16 // n, body, U['Q'])

    def middle_rows(k):
        n = U['nF']

        def body(c):
            p = 16 * k + c * n
            br = dot(a3[pl.ds(p, n)].reshape(n * 64, 128), w_eo[...])
            for r, a in enumerate(rows_of(br, n)):
                for q in range(4):
                    ln = slice(128 * q, 128 * q + 128)
                    m = src[p + r, :, ln].astype(F32) + (a[:, ln] * (1.0 / 64.0) + bias[6, :, ln])
                    act, slope = silu_parts(m)
                    mid[p + r, :, ln] = m
                    sl_mid[p + r, :, ln] = slope
                    d0[p + r, :, ln] = act.astype(BF16)
            pre = dot_t(d0[pl.ds(p, n)].reshape(n * 64, 512), w_df[...])
            for r, a in enumerate(rows_of(pre, n)):
                put_pair(y1, p + r + 1, hidden(a, 3, t1, p + r))
        loop(16 // n, body, U['F'])

    def result_rows():
        mk = mask[...].astype(F32)
        tall = jnp.sum(mk[:, 0:1])
        broad = jnp.sum(mk[0:1, :])
        sub = lax.broadcasted_iota(jnp.int32, (64, 128), 0)
        column = lax.rem(sub, 8) * 16 + 2 * (sub // 8)
        wi = broad.astype(jnp.int32)
        hi = tall.astype(jnp.int32)
        col_mask = [jnp.where(column + e < wi, 1.0, 0.0) for e in range(2)]
        n = U['nJ']

        def body(c):
            p = c * n
            acc = 0.0
            for i in range(3):
                acc = acc + dot_t(y3[pl.ds(p + i, n)].reshape(n * 64, 256), w_do[i])
            acc = acc.reshape(n, 64, 512)
            for r in range(n):
                m = mid[p + r]
                res = m + (acc[r] * (1.0 / 64.0) + bias[7])
                src[p + r] = res.astype(BF16)
                row_on = jnp.where(p + r < hi, 1.0, 0.0)
                for q in range(4):
                    ln = slice(q * 128, q * 128 + 128)
                    diff = res[:, ln] - tp[p + r, :, ln].astype(F32)
                    g = diff * (col_mask[q // 2] * row_on)
                    mid[p + r, :, ln] = g
                    eacc[...] += part_sum(g * diff)
                    g = g * (1.0 / 64.0)
                    g4[p + r + 1, :, ln] = g.astype(BF16)
                    bacc[7, :, ln] += part_sum(g)
        loop(32 // n, body, U['J'])
        return tall * broad

    def decoded_rows(k):
        def body(r):
            p = 8 * k + r
            a, b = to_natural(src[p].astype(F32), p % 4 if isinstance(p, int) else lax.rem(p, 4))
            decoded[p, :, 0:128] = a.astype(BF16)
            decoded[p, :, 128:256] = b.astype(BF16)
        loop(8, body, U['B'])
        return near(decoded.at[pl.ds(8 * k, 8)], decoded_h.at[pl.ds(8 * k, 8)], io_sem.at[2 + k])

    def back(x, slope_ref, row, b):
        g = x * slope_ref[row]
        bacc[b, :, 0:128] += part_sum(g)
        return g

    def dec_last_back():
        n = U['nC']

        def body(c):
            p = c * n
            acc = 0.0
            for i in range(3):
                acc = acc + dot(g4[pl.ds(p + i, n)].reshape(n * 64, 512), w_do[2 - i])
            for r, a in enumerate(rows_of(acc, n)):
                put_pair(zg, p + r + 1, back(a[:, :128] + folded(a[None, :, 128:])[0], t3, p + r, 5))
        loop(32 // n, body, U['K'])

    M = [3, 0, 1, 2]

    def dec_last_weights():
        gv = g4[pl.ds(1, 32)].reshape(2048, 512)
        cols = []
        for i in range(3):
            t = dot_p(gv, y3[pl.ds(i, 32)].reshape(2048, 256))
            for j in range(3):
                a, b = M[j] * 64, M[j + 1] * 64
                cols.append(t[0:256, a:a + 64] + t[256:512, b:b + 64])
        k_do = jnp.concatenate(cols, axis=1).astype(BF16)
        for a in range(dp):
            n = 576 // dp
            v = k_do[:, n * a:n * a + n]
            for b in range(4):
                for k in range(4):
                    at = spots[k][1]
                    r = 64 * b + 16 * k
                    part[2][a // 2, a % 2, b // 2, b % 2, :, at:at + n] = v[r:r + 16]

    def deal(name, k):
        g, at, n = spots[name]
        k = k.astype(BF16)
        for a in range(dp):
            v = k[:, n * a:n * a + n]
            for b in range(4):
                part[g][a // 2, a % 2, b // 2, b % 2, :, at:at + n] = v[16 * b:16 * b + 16]

    def quad_wgrad(z, g_ref, name):
        gq = jnp.concatenate([
            jnp.concatenate([g_ref[2 * r + 1, :, 0:128] for r in range(16)], axis=0),
            jnp.concatenate([g_ref[2 * r + 2, :, 0:128] for r in range(16)], axis=0)], axis=1)
        t = [dot_p(gq, quad_rows(z, 0, 16, d)) for d in range(4)]
        cols = []
        for i in range(3):
            s = t[i][0:128] + t[i + 1][128:256]
            for j in range(3):
                a, b = M[j] * 64, M[j + 1] * 64
                cols.append(s[0:64, a:a + 64] + s[64:128, b:b + 64])
        deal(name, jnp.concatenate(cols, axis=1))

    def quad_back(zin, v, slope_ref, b, zout):
        n = U['nQ']

        def body(c):
            acc = 0.0
            for d in range(4):
                acc = acc + dot(quad_rows(zin, c * n, n, d), v[d])
            for r, a in enumerate(rows_of(acc, n)):
                for e in range(2):
                    row = (c * n + r) * 2 + e
                    put_pair(zout, row + 1, back(a[:, 128 * e:128 * e + 128], slope_ref, row, b))
        loop(16 // n, body, U['Q'])

    def dec_first_weights():
        t = dot_p(zg[pl.ds(1, 32), :, 0:128].reshape(2048, 128), d0[...].reshape(2048, 512))
        deal("df", t[0:64, 0:256] + t[64:128, 256:512])

    def middle_back():
        n = U['nF']

        def body(c):
            p = c * n
            bk = dot(zg[pl.ds(p + 1, n), :, 0:128].reshape(n * 64, 128), w_df[...])
            for r, a in enumerate(rows_of(bk, n)):
                for q in range(4):
                    ln = slice(128 * q, 128 * q + 128)
                    gm = mid[p + r, :, ln] + sl_mid[p + r, :, ln] * a[:, ln]
                    mid[p + r, :, ln] = gm
                    g = gm * (1.0 / 64.0)
                    bacc[6, :, ln] += part_sum(g)
                    h4[p + r, :, ln] = g.astype(BF16)
            x = dot_t(h4[pl.ds(p, n)].reshape(n * 64, 512), w_eo[...])
            for r, a in enumerate(rows_of(x, n)):
                put_pair(zh, p + r + 1, back(a, s3, p + r, 2))
        loop(32 // n, body, U['F'])

    def enc_last_weights():
        t = dot_p(a3[...].reshape(2048, 128), h4[...].reshape(2048, 512))
        k = t[0:64, 0:256] + t[64:128, 256:512]
        g, at, n = spots["eo"]
        for a in range(dp):
            for b in range(4):
                v = eo_block(k[a * r_eo:a * r_eo + r_eo, 64 * b:64 * b + 64])
                part[g][a // 2, a % 2, b // 2, b % 2, :, at:at + n] = v.astype(BF16)

    def enc_first_weights(r0):
        gv = zh[pl.ds(1, 32)].reshape(2048, 256)
        g, at, n = spots["ef"]
        cols, done, sent = [], 0, 0
        for i in range(3):
            t = dot_p(gv, act0[pl.ds(i, 32)].reshape(2048, 512))
            cols.append((t[64:128, 0:256] + t[128:192, 256:512]).astype(BF16))
            cols.append((t[0:64, 0:256] + t[64:128, 256:512]).astype(BF16))
            cols.append((t[192:256, 0:256] + t[0:64, 256:512]).astype(BF16))
            k = jnp.concatenate(cols, axis=1)
            ready = dp * (i + 1) // 3
            for a in range(done, ready):
                v = k[:, n * a:n * a + n]
                for b in range(4):
                    part[g][a // 2, a % 2, b // 2, b % 2, :, at:at + n] = v[16 * b:16 * b + 16]
            done = ready
            r0.cores(i, sent, done // 2)
            sent = done // 2

    def deal_biases():
        sums = []
        for n in (0, 1, 2, 6, 3, 4, 5, 7):
            v = jnp.sum(bacc[n], axis=0, keepdims=True)
            sums.append(v[:, 0:256] + v[:, 256:512] if n >= 6 else v[:, 0:64] + v[:, 64:128])
        g, at, n = spots["bias"]
        for a in range(dp):
            v = bias_block([q[:, a * (q.shape[1] // dp):(a + 1) * (q.shape[1] // dp)] for q in sums]).astype(BF16)
            for b in range(4):
                part[g][a // 2, a % 2, b // 2, b % 2, :, at:at + n] = v

    def source_grad(k):
        n = U['nG']

        def body(c):
            p = 8 * k + c * n
            acc = 0.0
            for i in range(3):
                acc = acc + dot(zh[pl.ds(p + i, n)].reshape(n * 64, 256), w_ef[2 - i])
            acc = acc.reshape(n, 64, 512)
            for r in range(n):
                g = mid[p + r] + sl_src[p + r] * acc[r]
                a, b = to_natural(g, r % 4)
                images_grad[p + r, :, 0:128] = a.astype(BF16)
                images_grad[p + r, :, 128:256] = b.astype(BF16)
        loop(8 // n, body, U['Qr'])

    def source_grad_out(k):
        return near(images_grad.at[pl.ds(8 * k, 8)], images_grad_h.at[pl.ds(8 * k, 8)], image_sem.at[k])

    run = lambda name, f, *args: f(*args)
    for k in range(4):
        image_copies[k].wait()
        run('src%d' % k, source_rows, k)
    target_copy.wait()
    run('targets', target_rows)
    g1.square_one()
    g0.cores()
    g2.chips()
    g0.finish()
    g1.square_two()
    run('w0', first_weights)
    run('enc1', enc_first)
    g1.cores()
    run('enc2', quad_conv, z1, w_es, 1, s2, z2)
    g1.finish()
    run('w1', second_weights)
    run('enc3', quad_conv, z2, w_et, 2, s3, a3, False)
    run('middle', middle_rows, 0)
    g2.cores()
    run('middle', middle_rows, 1)
    g2.finish()
    run('w2', third_weights)
    run('dec2', quad_conv, y1, w_ds, 4, t2, y2)
    run('dec3', quad_conv, y2, w_dt, 5, t3, y3)
    mask_copy.wait()
    pixels = run('result', result_rows)
    loss[0] = 0.5 * jnp.sum(eacc[...]) / (pixels * 256.0)
    run('dec4b', dec_last_back)
    run('dec4w', dec_last_weights)
    run('dec3b', quad_back, zg, v_dt, t2, 4, zh)
    run('dec3w', quad_wgrad, y2, zg, "dt")
    run('dec2b', quad_back, zh, v_ds, t1, 3, zg)
    run('dec2w', quad_wgrad, y1, zh, "ds")
    r2 = DirectScatter(me, part[2], bufs2, *pairs[6:8])
    r2.cores(0, 0, nz)
    run('dec1w', dec_first_weights)
    run('midb', middle_back)
    r2.chips()
    run('enc4w', enc_last_weights)
    run('enc3w', quad_wgrad, z2, zh, "et")
    r1 = DirectScatter(me, part[1], bufs1, *pairs[8:10])
    r1.cores(0, 0, nz)
    run('enc3b', quad_back, zh, v_et, s2, 1, zg)
    r1.chips()
    run('enc2w', quad_wgrad, z1, zg, "es")
    run('enc2b', quad_back, zg, v_es, s1, 0, zh)
    run('bias', deal_biases)
    r0 = DirectScatter(me, part[0], bufs0, *pairs[10:12])
    run('enc1w', enc_first_weights, r0)
    out_copies = []
    for k in range(2):
        out_copies.append(run('out%d' % k, decoded_rows, k))
    r0.chips()
    for k in range(4):
        run('grad%d' % k, source_grad, k)
        out_copies.append(source_grad_out(k))
    for k in range(2, 4):
        out_copies.append(run('out%d' % k, decoded_rows, k))
    r2.finish(tot2)
    r1.finish(tot1)
    r0.finish(tot0)
    wait_all(out_copies)


def last_kernel(decoded_i, images_grad_i, loss_i, *refs):
    tots_i, (decoded, images_grad, loss), refs = refs[:3], refs[3:6], refs[6:]
    outs_h, refs = refs[:16], refs[16:]
    outs, tots, hold, sem, tot_sem, out_sem = refs[:16], refs[16:19], *refs[19:]
    dp = 64 // outs[3].shape[0]
    small = [pltpu.make_async_copy(p, q, tot_sem.at[k]) for k, (p, q) in enumerate(zip(tots_i, tots))]
    pairs = [(p, q, n * 2 + k, pl.ds(16 * k, 16)) for k in range(2) for n, (p, q) in enumerate(((decoded_i, decoded), (images_grad_i, images_grad)))]
    ins = [pltpu.make_async_copy(p.at[rows], hold.at[k], sem.at[k]) for p, q, k, rows in pairs]
    backs = [pltpu.make_async_copy(hold.at[k], q.at[rows], sem.at[4 + k]) for p, q, k, rows in pairs]
    for cp in small + ins:
        cp.start()
    loss[0] = loss_i[0]
    wait_all(small)
    spots, _ = places(dp)

    def piece(name):
        g, at, n = spots[name]
        return tots[g][:, at:at + n]
    for k, name in enumerate(("ef", "es", "et", None, "df", "ds", "dt")):
        if name:
            outs[k][...] = piece(name)
    outs[3][...] = piece("eo")[0:64 // dp]
    for k in range(4):
        outs[7][16 * k:16 * k + 16] = piece(k)
    for ref, v in zip(outs[8:], bias_rows(piece("bias"), 64 // dp)):
        ref[...] = v
    last = [pltpu.make_async_copy(p, q, out_sem.at[k]) for k, (p, q) in enumerate(zip(outs, outs_h))]
    for p, q in zip(ins, backs):
        p.wait()
        q.start()
    for cp in last:
        cp.start()
    wait_all(last + backs)


U = dict(B=4, nC=32, C=1, K=1, nQ=16, Q=1, nF=16, F=1, nJ=16, J=1, nG=8, Qr=1)


def per_device(images, targets, pixel_mask, ef, es, et, eo, eba, ebb, ebc, ebd, df, ds, dt, do, dba, dbb, dbc, dbd):
    dp = lax.axis_size("dp")
    nz = dp // 2
    widths = places(dp)[1]
    chips = len(chip_steps(nz))
    vm = pl.BlockSpec(memory_space=pltpu.VMEM)
    far = pl.BlockSpec(memory_space=pl.ANY)
    smem = pl.BlockSpec(memory_space=pltpu.SMEM)
    sem = pltpu.SemaphoreType.DMA
    V = lambda shape, dt: pltpu.VMEM(shape, dt)
    S = jax.ShapeDtypeStruct
    args = [images[0], targets[0], pixel_mask[0], ef.T, es.T, et.T, eo, df.T, ds.T, dt.T, do.T]
    args += [b.reshape(1, -1) for b in (eba, ebb, ebc, ebd, dba, dbb, dbc, dbd)]
    sums = []
    for w in widths:
        sums += [V((nz, 2, 2, 16, w), BF16)] * 2 + [V((chips, 16, w), BF16)]
    big = S((32, 128, 256), BF16)
    tots = [S((16, w), F32) for w in widths]
    decoded, images_grad, loss, *kept = pl.pallas_call(
        functools.partial(main_kernel, U),
        out_shape=[big, big, S((1,), F32), *tots],
        in_specs=[far] * 19, out_specs=[far, far, smem, vm, vm, vm],
        scratch_shapes=[V(a.shape, a.dtype) for a in args] + [
            V((32, 64, 512), BF16), V((34, 64, 512), BF16), V((32, 64, 512), F32),
            V((34, 64, 256), BF16), V((34, 64, 256), BF16), V((32, 64, 128), BF16),
            V((34, 64, 256), BF16), V((34, 64, 256), BF16), V((34, 64, 256), BF16)] + [V((32, 64, 128), F32)] * 6 + [
            V((32, 64, 512), F32), V((32, 64, 512), F32), V((32, 64, 512), BF16),
            V((34, 64, 512), BF16), V((32, 64, 512), BF16), V((34, 64, 256), BF16), V((34, 64, 256), BF16),
            V((4, 2, 128, 128), F32),
            V((3, 256, 512), BF16)] + [V((4, 256, 256), BF16)] * 8 + [
            V((3, 512, 256), BF16), V((128, 512), BF16), V((128, 512), BF16),
            V((8, 1, 512), F32), V((8, 8, 512), F32), V((8, 128), F32), V((32, 64, 512), BF16)]
        + [V((nz, 2, 2, 2, 16, w), BF16) for w in widths] * 2 + sums
        + [sem((16,)), sem((4,)), sem((6,))] + [sem((chips + nz,))] * 2 + [sem((nz + 4,))] * 2 + [sem((chips + nz,))] * 2 + [sem((chips + 3,))] * 6,
        compiler_params=pltpu.CompilerParams(collective_id=0, has_side_effects=True, vmem_limit_bytes=63 * 2**20),
    )(*args)
    f = lambda *s: S(s, F32)
    grads = [f(16, 2304 // dp), f(16, 576 // dp), f(16, 576 // dp), f(64 // dp, 64), f(16, 256 // dp),
             f(16, 576 // dp), f(16, 576 // dp), f(64, 576 // dp)] + [f(1, s // dp) for s in (64, 64, 64, 256) * 2]
    outs = pl.pallas_call(
        last_kernel,
        out_shape=[big, big, S((1,), F32)] + grads,
        in_specs=[far, far, smem, far, far, far], out_specs=[far, far, smem] + [far] * 16,
        scratch_shapes=[V(g.shape, F32) for g in grads + tots] + [V((4, 16, 128, 256), BF16), sem((8,)), sem((3,)), sem((16,))],
        compiler_params=pltpu.CompilerParams(vmem_limit_bytes=60 * 2**20),
    )(decoded, images_grad, loss, *kept)
    decoded, images_grad, loss, g_ef, g_es, g_et, g_eo, g_df, g_ds, g_dt, g_do = outs[:11]
    bs = [b.reshape(-1) for b in outs[11:]]
    return (decoded[None], images_grad[None], loss, g_ef.T, g_es.T, g_et.T, g_eo, *bs[:4],
            g_df.T, g_ds.T, g_dt.T, g_do.T, *bs[4:])


def solution(mesh):
    img, w, b = P(("dp", "fsdp"), None, None, None), P("dp", "fsdp"), P("dp")
    placed = (img, img, P(("dp", "fsdp"), None, None)) + (w,) * 4 + (b,) * 4 + (w,) * 4 + (b,) * 4
    return jax.shard_map(
        per_device, mesh=mesh, in_specs=placed,
        out_specs=(img, img, P(("dp", "fsdp"))) + (w,) * 4 + (b,) * 4 + (w,) * 4 + (b,) * 4,
        check_vma=False)
```

```python
import functools
import jax
import jax.numpy as jnp
from jax import lax
from jax.experimental import pallas as pl
from jax.experimental.pallas import tpu as pltpu
from jax.sharding import PartitionSpec as P

F32, BF16 = jnp.float32, jnp.bfloat16
MESH = pl.DeviceIdType.MESH


def dot(a, b):
    return jnp.dot(a, b, preferred_element_type=F32)


def dot_t(a, b):
    return lax.dot_general(a, b, (((1,), (1,)), ((), ())), preferred_element_type=F32)


def dot_p(a, b):
    return lax.dot_general(a, b, (((0,), (0,)), ((), ())), preferred_element_type=F32)


def loop(count, body, unroll):
    if unroll >= count:
        for c in range(count):
            body(c)
    else:
        def step(k, _):
            for u in range(unroll):
                body(k * unroll + u)
            return 0
        lax.fori_loop(0, count // unroll, step, 0)


def masks():
    lane = lax.broadcasted_iota(jnp.int32, (1, 1, 8, 128), 3)
    row = lax.broadcasted_iota(jnp.int32, (1, 1, 8, 128), 2)
    return lane < 64, row


def shifted(x):
    n = x.shape[0]
    _, row = masks()
    x4 = x.reshape(n, 8, 8, 128)
    nxt = jnp.where(row == 7, 0.0, pltpu.roll(x4[:, :1], 7, 2))
    prv = jnp.where(row == 0, 0.0, pltpu.roll(x4[:, 7:], 1, 2))
    up = jnp.concatenate([x4[:, 1:], nxt], axis=1)
    dn = jnp.concatenate([prv, x4[:, :7]], axis=1)
    return up, dn


def beside(x):
    lo, _ = masks()
    up, dn = shifted(x)
    return jnp.where(lo, up, dn).reshape(x.shape)


def folded(x):
    lo, _ = masks()
    up, dn = shifted(x)
    return jnp.where(lo, dn, up).reshape(x.shape)


def silu_parts(v):
    h = 0.5 * v
    u = 1.0 + jnp.tanh(h)
    act = h * u
    w = 0.5 * u
    return act, w + act * (1.0 - w)


def part_sum(x):
    return x.reshape(-1, 8, x.shape[-1]).sum(axis=0)


def put_pair(ref, idx, x):
    ref[idx, :, 0:128] = x.astype(BF16)
    ref[idx, :, 128:256] = beside(x[None])[0].astype(BF16)


def quad_rows(ref, r0, n, d):
    return jnp.concatenate([ref[2 * (r0 + k) + d] for k in range(n)], axis=0)


def rows_of(x, n):
    return [x[64 * r:64 * r + 64] for r in range(n)]


def stack_in(k):
    z = jnp.zeros_like(k[0])
    rows = ((k[1], k[2]), (k[0], k[1]), (z, k[0]), (k[2], z))
    return jnp.concatenate([jnp.concatenate(r, axis=1) for r in rows], axis=0)


def stack_out(k):
    z = jnp.zeros_like(k[0])
    rows = ((k[1], k[2], z, k[0]), (k[0], k[1], k[2], z))
    return jnp.concatenate([jnp.concatenate(r, axis=1) for r in rows], axis=0)


TAPS = ("ef", "es", "et", "df", "ds", "dt")
ROWS = dict(ef=2304, es=576, et=576, df=256, ds=576, dt=576, do=576)


def places(dp):
    groups = ((("ef", 2304 // dp), ("es", 576 // dp), ("bias", 128 // dp)),
              (("et", 576 // dp), ("df", 256 // dp), ("eo", 64)),
              (("ds", 576 // dp), ("dt", 576 // dp)) + tuple((k, 576 // dp) for k in range(4)))
    spots, widths = {}, []
    for g, group in enumerate(groups):
        at = 0
        for name, n in group:
            spots[name] = (g, at, n)
            at += n
        widths.append(at + (-at % 128))
    return spots, widths


def bias_block(parts):
    w = parts[3].shape[1] // 2
    n = parts[0].shape[1]
    fill = lambda v: jnp.concatenate([v, jnp.zeros((1, w - n), F32)], axis=1)
    rows = [fill(parts[k]) for k in (0, 1, 2, 4, 5, 6)]
    for k in (3, 7):
        rows += [parts[k][:, :w], parts[k][:, w:]]
    return jnp.concatenate(rows + [jnp.zeros((6, w), F32)], axis=0)


def bias_rows(block, n):
    thin = [block[k:k + 1, :n] for k in range(6)]
    wide = [jnp.concatenate([block[k:k + 1], block[k + 1:k + 2]], axis=1) for k in (6, 8)]
    return thin[:3] + wide[:1] + thin[3:] + wide[1:]


def eo_block(eo):
    return jnp.concatenate([eo, jnp.zeros((16 - eo.shape[0], 64), F32)], axis=0)


def lanes_to(parts, wide):
    at = sum(p.shape[1] for p in parts)
    if at < wide:
        parts = parts + [jnp.zeros((parts[0].shape[0], wide - at), parts[0].dtype)]
    return jnp.concatenate(parts, axis=1)


def where_am_i():
    a, b = lax.axis_index("dp"), lax.axis_index("fsdp")
    return a // 2, lax.rem(a, 2), b // 2, lax.rem(b, 2)


def device(z, y, x, c):
    return (z * 2 + y, x * 2 + c)


def far_copy(src, dst, send, recv, to):
    cp = pltpu.make_async_remote_copy(
        src_ref=src, dst_ref=dst, send_sem=send, recv_sem=recv, device_id=to, device_id_type=MESH)
    cp.start()
    return cp


def wait_all(copies):
    for cp in copies:
        cp.wait()


class Gather:
    def __init__(self, me, buf, send, recv):
        self.me, self.buf, self.send, self.recv = me, buf, send, recv
        self.nz = buf.shape[0]
        self.h = self.nz // 2

    def copy(self, view, k, to):
        return far_copy(view, view, self.send.at[k], self.recv.at[k], device(*to))

    def along_z(self):
        z, y, x, c = self.me
        mine = self.buf.at[z, y, x, c]
        self.fly = [self.copy(mine, 3 + k, (lax.rem(z + k, self.nz), y, x, c)) for k in range(1, self.nz)]

    def square_one(self):
        z, y, x, c = self.me
        wait_all(self.fly)
        lo, hi = pl.ds(0, self.h), pl.ds(self.h, self.nz - self.h)
        self.fly = [self.copy(self.buf.at[lo, y, x, c], 0, (z, 1 - y, x, c)),
                    self.copy(self.buf.at[hi, y, x, c], 1, (z, y, 1 - x, c))]

    def square_two(self):
        z, y, x, c = self.me
        wait_all(self.fly)
        lo, hi = pl.ds(0, self.h), pl.ds(self.h, self.nz - self.h)
        self.fly = [self.copy(self.buf.at[lo, :, x, c], 2, (z, y, 1 - x, c)),
                    self.copy(self.buf.at[hi, y, :, c], 3, (z, 1 - y, x, c))]

    def cores(self):
        z, y, x, c = self.me
        wait_all(self.fly)
        self.fly = [self.copy(self.buf.at[:, :, :, c], self.nz + 3, (z, y, x, 1 - c))]

    def finish(self):
        wait_all(self.fly)


class DirectGather:
    def __init__(self, me, buf, send, recv):
        self.me, self.buf, self.send, self.recv = me, buf, send, recv
        self.nz = buf.shape[0]
        self.steps = chip_steps(self.nz)

    def copy(self, view, k, to):
        return far_copy(view, view, self.send.at[k], self.recv.at[k], device(*to))

    def chips(self):
        z, y, x, c = self.me
        mine = self.buf.at[z, y, x, c]
        self.fly = {}
        for k, step in reversed(list(enumerate(self.steps))):
            self.fly[k] = self.copy(mine, k, other_chip(self.me, step, self.nz))

    def cores(self):
        z, y, x, c = self.me
        self.last = []
        for dz in range(self.nz):
            wait_all([self.fly[k] for k, step in enumerate(self.steps) if step[0] == dz])
            rows = self.buf.at[lax.rem(z + self.nz - dz, self.nz), :, :, c]
            self.last.append(self.copy(rows, len(self.steps) + dz, (z, y, x, 1 - c)))

    def finish(self):
        wait_all(self.last)


class DirectScatter:
    def __init__(self, me, part, bufs, send, recv):
        self.me, self.part, self.send, self.recv = me, part, send, recv
        self.in1, self.s1, self.in2 = bufs
        self.nz = part.shape[0]
        self.steps = chip_steps(self.nz)
        self.fly = []

    def copy(self, src, dst, k, to):
        return far_copy(src, dst, self.send.at[k], self.recv.at[k], device(*to))

    def cores(self, k, lo, hi):
        z, y, x, c = self.me
        rows = pl.ds(lo, hi - lo)
        self.fly.append(self.copy(self.part.at[rows, :, :, 1 - c], self.in1.at[rows], len(self.steps) + k, (z, y, x, 1 - c)))

    def chips(self):
        z, y, x, c = self.me
        wait_all(self.fly)
        for k in range(self.nz):
            self.s1[k] = add16(self.part[k, :, :, c], self.in1[k])
        self.fly = []
        for k, step in reversed(list(enumerate(self.steps))):
            to = other_chip(self.me, step, self.nz)
            self.fly.append(self.copy(self.s1.at[to[0], to[1], to[2]], self.in2.at[k], k, to))

    def finish(self, out):
        z, y, x, c = self.me
        wait_all(self.fly)
        total = self.s1[z, y, x].astype(F32)
        for k in range(len(self.steps)):
            total = total + self.in2[k].astype(F32)
        out[...] = total


def chip_steps(nz):
    return [(dz, dy, dx) for dz in range(nz) for dy in range(2) for dx in range(2)][1:]


def other_chip(me, step, nz):
    z, y, x, c = me
    return (lax.rem(z + step[0], nz), lax.rem(y + step[1], 2), lax.rem(x + step[2], 2), c)


def add16(p, q):
    return (p.astype(F32) + q.astype(F32)).astype(BF16)


def main_kernel(U, *refs):
    (images_h, targets_h, mask_h, ef_h, es_h, et_h, eo_h, df_h, ds_h, dt_h, do_h, *rest) = refs
    biases_h, rest = rest[:8], rest[8:]
    (decoded_h, images_grad_h, loss, tot0, tot1, tot2,
     images, targets, mask, ef_s, es_s, et_s, eo_s, df_s, ds_s, dt_s, do_s, *rest) = rest
    biases_s, rest = rest[:8], rest[8:]
    decoded, images_grad = images, targets
    (src, act0, sl_src, z1, z2, a3, y1, y2, y3, s1, s2, s3, t1, t2, t3,
     mid, sl_mid, d0, g4, h4, zg, zh, stage,
     w_ef, w_es, w_et, v_es, v_et, w_ds, w_dt, v_ds, v_dt, w_do, w_eo, w_df, bias, bacc, eacc, tp,
     *rest) = rest
    whole, part, rest = rest[:3], rest[3:6], rest[6:]
    bufs0, bufs1, bufs2, rest = rest[:3], rest[3:6], rest[6:9], rest[9:]
    shard_sem, image_sem, io_sem, *pairs = rest

    nz = whole[0].shape[0]
    dp = nz * 2
    spots, widths = places(dp)
    me = where_am_i()
    z, y, x, c = me

    barrier = pltpu.get_barrier_semaphore()
    others = [device(*other_chip(me, step, nz)) for step in chip_steps(nz)] + [device(z, y, x, 1 - c)]
    for d in others:
        pl.semaphore_signal(barrier, inc=1, device_id=d, device_id_type=MESH)

    def near(src, dst, sem):
        cp = pltpu.make_async_copy(src, dst, sem)
        cp.start()
        return cp
    shards_h = (ef_h, es_h, et_h, eo_h, df_h, ds_h, dt_h, do_h, *biases_h)
    shards_s = (ef_s, es_s, et_s, eo_s, df_s, ds_s, dt_s, do_s, *biases_s)
    shard_copies = [near(p, q, shard_sem.at[k]) for k, (p, q) in enumerate(zip(shards_h, shards_s))]
    image_copies = [near(images_h.at[pl.ds(8 * k, 8)], images.at[pl.ds(8 * k, 8)], image_sem.at[k]) for k in range(4)]
    target_copy = near(targets_h, targets, io_sem.at[0])
    mask_copy = near(mask_h, mask, io_sem.at[1])

    g0 = DirectGather(me, whole[0], *pairs[0:2])
    g1 = Gather(me, whole[1], *pairs[2:4])
    g2 = DirectGather(me, whole[2], *pairs[4:6])
    wait_all(shard_copies)
    bias_part = bias_block([b[...].astype(F32) for b in biases_s]).astype(BF16)
    whole[0][z, y, x, c] = lanes_to([ef_s[...], es_s[...], bias_part], widths[0])
    pl.semaphore_wait(barrier, len(others))
    g0.chips()
    whole[1][z, y, x, c] = lanes_to([et_s[...], df_s[...], eo_block(eo_s[...].astype(F32)).astype(BF16)], widths[1])
    whole[2][z, y, x, c] = lanes_to([ds_s[...], dt_s[...]] + [do_s[16 * k:16 * k + 16] for k in range(4)], widths[2])
    g1.along_z()

    for ref in (act0, g4, z1, z2, y1, y2, y3, zg, zh):
        ref[0] = jnp.zeros(ref.shape[1:], ref.dtype)
        ref[33] = jnp.zeros(ref.shape[1:], ref.dtype)
    bacc[...] = jnp.zeros_like(bacc)
    eacc[...] = jnp.zeros_like(eacc)

    def blocks(name):
        g, at, n = spots[name]
        return [[whole[g][a // 2, a % 2, b // 2, b % 2, :, at:at + n] for b in range(4)] for a in range(dp)]

    def across(name):
        return jnp.concatenate([jnp.concatenate(col, axis=0) for col in blocks(name)], axis=1)

    def tap(k, i, n):
        return [k[:, (3 * i + j) * n:(3 * i + j + 1) * n] for j in range(3)]

    def quad_weights(k, w_ref, v_ref):
        w_ref[0, 128:256, :] = jnp.zeros((128, 256), BF16)
        w_ref[3, 0:128, :] = jnp.zeros((128, 256), BF16)
        v_ref[0, :, 128:256] = jnp.zeros((256, 128), BF16)
        v_ref[3, :, 0:128] = jnp.zeros((256, 128), BF16)
        for i in range(3):
            t = tap(k, i, 64)
            f = stack_out(t)
            w_ref[i, 0:128, :] = f
            w_ref[i + 1, 128:256, :] = f
            b = stack_in(t)
            v_ref[2 - i, :, 0:128] = b
            v_ref[3 - i, :, 128:256] = b

    def two(k):
        z = jnp.zeros_like(k)
        return jnp.concatenate([jnp.concatenate([k, z], axis=1), jnp.concatenate([z, k], axis=1)], axis=0)

    r_eo = 64 // dp

    def first_weights():
        k = across("ef")
        for i in range(3):
            w_ef[i] = stack_in(tap(k, i, 256))
        rows = [bias_rows(col[0].astype(F32), 64 // dp) for col in blocks("bias")]
        for n, k in enumerate((0, 1, 2, 4, 5, 6, 3, 7)):
            v = jnp.concatenate([r[k] for r in rows], axis=1)
            v = jnp.concatenate([v, v], axis=1)
            if n < 6:
                bias[n, :, 0:128] = v
            else:
                bias[n] = v * (1.0 / 64.0)
        quad_weights(across("es"), w_es, v_es)

    def second_weights():
        quad_weights(across("et"), w_et, v_et)
        w_eo[...] = two(jnp.concatenate([
            jnp.concatenate([blk.astype(F32)[0:r_eo] for blk in col], axis=1) for col in blocks("eo")], axis=0).astype(BF16))
        w_df[...] = two(across("df"))

    def third_weights():
        quad_weights(across("ds"), w_ds, v_ds)
        quad_weights(across("dt"), w_dt, v_dt)
        quarter = [across(k) for k in range(4)]
        k = jnp.concatenate([quarter[k][16 * b:16 * b + 16] for b in range(4) for k in range(4)], axis=0)
        for i in range(3):
            w_do[i] = stack_out(tap(k, i, 64))

    def to_pairs(v, slot):
        stage[slot, 0] = v[:, :128]
        stage[slot, 1] = v[:, 128:]
        return [jnp.concatenate([stage[slot, h, pl.ds(2 * t + e, 8, stride=16), :] for t in range(8)], axis=0)
                for e in range(2) for h in range(2)]

    def to_natural(v, slot):
        for e in range(2):
            for h in range(2):
                for t in range(8):
                    stage[slot, h, pl.ds(2 * t + e, 8, stride=16), :] = v[8 * t:8 * t + 8, e * 256 + h * 128:e * 256 + h * 128 + 128]
        return stage[slot, 0], stage[slot, 1]

    def source_rows(k):
        def body(r):
            p = 8 * k + r
            v = images[p].astype(F32)
            slot = p % 4 if isinstance(p, int) else lax.rem(p, 4)
            for q, x in enumerate(to_pairs(v, slot)):
                ln = slice(q * 128, q * 128 + 128)
                act, slope = silu_parts(x)
                src[p, :, ln] = x.astype(BF16)
                act0[p + 1, :, ln] = act.astype(BF16)
                sl_src[p, :, ln] = slope
        loop(8, body, U['B'])

    def target_rows():
        def body(p):
            slot = p % 4 if isinstance(p, int) else lax.rem(p, 4)
            for q, t in enumerate(to_pairs(targets[p].astype(F32), slot)):
                tp[p, :, q * 128:q * 128 + 128] = t.astype(BF16)
        loop(32, body, U['B'])

    def hidden(pre, b, slope_ref, row):
        act, slope = silu_parts(pre + bias[b, :, 0:128])
        slope_ref[row] = slope
        return act

    def enc_first():
        n = U['nC']

        def body(c):
            p = c * n
            acc = 0.0
            for i in range(3):
                acc = acc + dot_t(act0[pl.ds(p + i, n)].reshape(n * 64, 512), w_ef[i])
            for r, a in enumerate(rows_of(acc, n)):
                put_pair(z1, p + r + 1, hidden(a[:, :128] + folded(a[None, :, 128:])[0], 0, s1, p + r))
        loop(32 // n, body, U['C'])

    def quad_conv(zin, w, b, slope_ref, zout, pair=True):
        n = U['nQ']

        def body(c):
            acc = 0.0
            for d in range(4):
                acc = acc + dot_t(quad_rows(zin, c * n, n, d), w[d])
            for r, a in enumerate(rows_of(acc, n)):
                for e in range(2):
                    row = (c * n + r) * 2 + e
                    act = hidden(a[:, 128 * e:128 * e + 128], b, slope_ref, row)
                    if pair:
                        put_pair(zout, row + 1, act)
                    else:
                        zout[row] = act.astype(BF16)
        loop(16 // n, body, U['Q'])

    def middle_rows(k):
        n = U['nF']

        def body(c):
            p = 16 * k + c * n
            br = dot(a3[pl.ds(p, n)].reshape(n * 64, 128), w_eo[...])
            for r, a in enumerate(rows_of(br, n)):
                for q in range(4):
                    ln = slice(128 * q, 128 * q + 128)
                    m = src[p + r, :, ln].astype(F32) + (a[:, ln] * (1.0 / 64.0) + bias[6, :, ln])
                    act, slope = silu_parts(m)
                    mid[p + r, :, ln] = m
                    sl_mid[p + r, :, ln] = slope
                    d0[p + r, :, ln] = act.astype(BF16)
            pre = dot_t(d0[pl.ds(p, n)].reshape(n * 64, 512), w_df[...])
            for r, a in enumerate(rows_of(pre, n)):
                put_pair(y1, p + r + 1, hidden(a, 3, t1, p + r))
        loop(16 // n, body, U['F'])

    def result_rows():
        mk = mask[...].astype(F32)
        tall = jnp.sum(mk[:, 0:1])
        broad = jnp.sum(mk[0:1, :])
        sub = lax.broadcasted_iota(jnp.int32, (64, 128), 0)
        column = lax.rem(sub, 8) * 16 + 2 * (sub // 8)
        wi = broad.astype(jnp.int32)
        hi = tall.astype(jnp.int32)
        col_mask = [jnp.where(column + e < wi, 1.0, 0.0) for e in range(2)]
        n = U['nJ']

        def body(c):
            p = c * n
            acc = 0.0
            for i in range(3):
                acc = acc + dot_t(y3[pl.ds(p + i, n)].reshape(n * 64, 256), w_do[i])
            acc = acc.reshape(n, 64, 512)
            for r in range(n):
                m = mid[p + r]
                res = m + (acc[r] * (1.0 / 64.0) + bias[7])
                src[p + r] = res.astype(BF16)
                row_on = jnp.where(p + r < hi, 1.0, 0.0)
                for q in range(4):
                    ln = slice(q * 128, q * 128 + 128)
                    diff = res[:, ln] - tp[p + r, :, ln].astype(F32)
                    g = diff * (col_mask[q // 2] * row_on)
                    mid[p + r, :, ln] = g
                    eacc[...] += part_sum(g * diff)
                    g = g * (1.0 / 64.0)
                    g4[p + r + 1, :, ln] = g.astype(BF16)
                    bacc[7, :, ln] += part_sum(g)
        loop(32 // n, body, U['J'])
        return tall * broad

    def decoded_rows(k):
        def body(r):
            p = 8 * k + r
            a, b = to_natural(src[p].astype(F32), p % 4 if isinstance(p, int) else lax.rem(p, 4))
            decoded[p, :, 0:128] = a.astype(BF16)
            decoded[p, :, 128:256] = b.astype(BF16)
        loop(8, body, U['B'])
        return near(decoded.at[pl.ds(8 * k, 8)], decoded_h.at[pl.ds(8 * k, 8)], io_sem.at[2 + k])

    def back(x, slope_ref, row, b):
        g = x * slope_ref[row]
        bacc[b, :, 0:128] += part_sum(g)
        return g

    def dec_last_back():
        n = U['nC']

        def body(c):
            p = c * n
            acc = 0.0
            for i in range(3):
                acc = acc + dot(g4[pl.ds(p + i, n)].reshape(n * 64, 512), w_do[2 - i])
            for r, a in enumerate(rows_of(acc, n)):
                put_pair(zg, p + r + 1, back(a[:, :128] + folded(a[None, :, 128:])[0], t3, p + r, 5))
        loop(32 // n, body, U['K'])

    M = [3, 0, 1, 2]

    def dec_last_weights():
        gv = g4[pl.ds(1, 32)].reshape(2048, 512)
        cols = []
        for i in range(3):
            t = dot_p(gv, y3[pl.ds(i, 32)].reshape(2048, 256))
            for j in range(3):
                a, b = M[j] * 64, M[j + 1] * 64
                cols.append(t[0:256, a:a + 64] + t[256:512, b:b + 64])
        k_do = jnp.concatenate(cols, axis=1).astype(BF16)
        for a in range(dp):
            n = 576 // dp
            v = k_do[:, n * a:n * a + n]
            for b in range(4):
                for k in range(4):
                    at = spots[k][1]
                    r = 64 * b + 16 * k
                    part[2][a // 2, a % 2, b // 2, b % 2, :, at:at + n] = v[r:r + 16]

    def deal(name, k):
        g, at, n = spots[name]
        k = k.astype(BF16)
        for a in range(dp):
            v = k[:, n * a:n * a + n]
            for b in range(4):
                part[g][a // 2, a % 2, b // 2, b % 2, :, at:at + n] = v[16 * b:16 * b + 16]

    def quad_wgrad(z, g_ref, name):
        gq = jnp.concatenate([
            jnp.concatenate([g_ref[2 * r + 1, :, 0:128] for r in range(16)], axis=0),
            jnp.concatenate([g_ref[2 * r + 2, :, 0:128] for r in range(16)], axis=0)], axis=1)
        t = [dot_p(gq, quad_rows(z, 0, 16, d)) for d in range(4)]
        cols = []
        for i in range(3):
            s = t[i][0:128] + t[i + 1][128:256]
            for j in range(3):
                a, b = M[j] * 64, M[j + 1] * 64
                cols.append(s[0:64, a:a + 64] + s[64:128, b:b + 64])
        deal(name, jnp.concatenate(cols, axis=1))

    def quad_back(zin, v, slope_ref, b, zout):
        n = U['nQ']

        def body(c):
            acc = 0.0
            for d in range(4):
                acc = acc + dot(quad_rows(zin, c * n, n, d), v[d])
            for r, a in enumerate(rows_of(acc, n)):
                for e in range(2):
                    row = (c * n + r) * 2 + e
                    put_pair(zout, row + 1, back(a[:, 128 * e:128 * e + 128], slope_ref, row, b))
        loop(16 // n, body, U['Q'])

    def dec_first_weights():
        t = dot_p(zg[pl.ds(1, 32), :, 0:128].reshape(2048, 128), d0[...].reshape(2048, 512))
        deal("df", t[0:64, 0:256] + t[64:128, 256:512])

    def middle_back():
        n = U['nN']

        def body(c):
            p = c * n
            bk = dot(zg[pl.ds(p + 1, n), :, 0:128].reshape(n * 64, 128), w_df[...])
            for r, a in enumerate(rows_of(bk, n)):
                for q in range(4):
                    ln = slice(128 * q, 128 * q + 128)
                    gm = mid[p + r, :, ln] + sl_mid[p + r, :, ln] * a[:, ln]
                    mid[p + r, :, ln] = gm
                    g = gm * (1.0 / 64.0)
                    bacc[6, :, ln] += part_sum(g)
                    h4[p + r, :, ln] = g.astype(BF16)
            x = dot_t(h4[pl.ds(p, n)].reshape(n * 64, 512), w_eo[...])
            for r, a in enumerate(rows_of(x, n)):
                put_pair(zh, p + r + 1, back(a, s3, p + r, 2))
        loop(32 // n, body, U['F'])

    def enc_last_weights():
        t = dot_p(a3[...].reshape(2048, 128), h4[...].reshape(2048, 512))
        k = t[0:64, 0:256] + t[64:128, 256:512]
        g, at, n = spots["eo"]
        for a in range(dp):
            for b in range(4):
                v = eo_block(k[a * r_eo:a * r_eo + r_eo, 64 * b:64 * b + 64])
                part[g][a // 2, a % 2, b // 2, b % 2, :, at:at + n] = v.astype(BF16)

    def enc_first_weights(r0):
        gv = zh[pl.ds(1, 32)].reshape(2048, 256)
        g, at, n = spots["ef"]
        cols, done, sent = [], 0, 0
        for i in range(3):
            t = dot_p(gv, act0[pl.ds(i, 32)].reshape(2048, 512))
            cols.append((t[64:128, 0:256] + t[128:192, 256:512]).astype(BF16))
            cols.append((t[0:64, 0:256] + t[64:128, 256:512]).astype(BF16))
            cols.append((t[192:256, 0:256] + t[0:64, 256:512]).astype(BF16))
            k = jnp.concatenate(cols, axis=1)
            ready = dp * (i + 1) // 3
            for a in range(done, ready):
                v = k[:, n * a:n * a + n]
                for b in range(4):
                    part[g][a // 2, a % 2, b // 2, b % 2, :, at:at + n] = v[16 * b:16 * b + 16]
            done = ready
            r0.cores(i, sent, done // 2)
            sent = done // 2

    def deal_biases():
        sums = []
        for n in (0, 1, 2, 6, 3, 4, 5, 7):
            v = jnp.sum(bacc[n], axis=0, keepdims=True)
            sums.append(v[:, 0:256] + v[:, 256:512] if n >= 6 else v[:, 0:64] + v[:, 64:128])
        g, at, n = spots["bias"]
        for a in range(dp):
            v = bias_block([q[:, a * (q.shape[1] // dp):(a + 1) * (q.shape[1] // dp)] for q in sums]).astype(BF16)
            for b in range(4):
                part[g][a // 2, a % 2, b // 2, b % 2, :, at:at + n] = v

    def source_grad(k):
        n = U['nG']

        def body(c):
            p = 16 * k + c * n
            acc = 0.0
            for i in range(3):
                acc = acc + dot(zh[pl.ds(p + i, n)].reshape(n * 64, 256), w_ef[2 - i])
            acc = acc.reshape(n, 64, 512)
            for r in range(n):
                g = mid[p + r] + sl_src[p + r] * acc[r]
                a, b = to_natural(g, r % 4)
                images_grad[p + r, :, 0:128] = a.astype(BF16)
                images_grad[p + r, :, 128:256] = b.astype(BF16)
        loop(16 // n, body, U['Qr'])

    def source_grad_out(k):
        return near(images_grad.at[pl.ds(16 * k, 16)], images_grad_h.at[pl.ds(16 * k, 16)], image_sem.at[k])

    run = lambda name, f, *args: f(*args)
    for k in range(4):
        image_copies[k].wait()
        run('src%d' % k, source_rows, k)
    target_copy.wait()
    run('targets', target_rows)
    g1.square_one()
    g0.cores()
    g2.chips()
    g0.finish()
    g1.square_two()
    run('w0', first_weights)
    run('enc1', enc_first)
    g1.cores()
    run('enc2', quad_conv, z1, w_es, 1, s2, z2)
    g1.finish()
    run('w1', second_weights)
    run('enc3', quad_conv, z2, w_et, 2, s3, a3, False)
    run('middle', middle_rows, 0)
    g2.cores()
    run('middle', middle_rows, 1)
    g2.finish()
    run('w2', third_weights)
    run('dec2', quad_conv, y1, w_ds, 4, t2, y2)
    run('dec3', quad_conv, y2, w_dt, 5, t3, y3)
    mask_copy.wait()
    pixels = run('result', result_rows)
    loss[0] = 0.5 * jnp.sum(eacc[...]) / (pixels * 256.0)
    run('dec4b', dec_last_back)
    run('dec4w', dec_last_weights)
    run('dec3b', quad_back, zg, v_dt, t2, 4, zh)
    run('dec3w', quad_wgrad, y2, zg, "dt")
    run('dec2b', quad_back, zh, v_ds, t1, 3, zg)
    run('dec2w', quad_wgrad, y1, zh, "ds")
    r2 = DirectScatter(me, part[2], bufs2, *pairs[6:8])
    r2.cores(0, 0, nz)
    run('dec1w', dec_first_weights)
    run('midb', middle_back)
    r2.chips()
    run('enc4w', enc_last_weights)
    run('enc3w', quad_wgrad, z2, zh, "et")
    r1 = DirectScatter(me, part[1], bufs1, *pairs[8:10])
    r1.cores(0, 0, nz)
    run('enc3b', quad_back, zh, v_et, s2, 1, zg)
    r1.chips()
    run('enc2w', quad_wgrad, z1, zg, "es")
    run('enc2b', quad_back, zg, v_es, s1, 0, zh)
    run('bias', deal_biases)
    r0 = DirectScatter(me, part[0], bufs0, *pairs[10:12])
    run('enc1w', enc_first_weights, r0)
    out_copies = []
    for k in range(2):
        out_copies.append(run('out%d' % k, decoded_rows, k))
    r0.chips()
    for k in range(2):
        run('grad%d' % k, source_grad, k)
        out_copies.append(source_grad_out(k))
    for k in range(2, 4):
        out_copies.append(run('out%d' % k, decoded_rows, k))
    r2.finish(tot2)
    r1.finish(tot1)
    r0.finish(tot0)
    wait_all(out_copies)


def last_kernel(decoded_i, images_grad_i, loss_i, *refs):
    tots_i, (decoded, images_grad, loss), refs = refs[:3], refs[3:6], refs[6:]
    outs_h, refs = refs[:16], refs[16:]
    outs, tots, hold, sem, tot_sem, out_sem = refs[:16], refs[16:19], *refs[19:]
    dp = 64 // outs[3].shape[0]
    small = [pltpu.make_async_copy(p, q, tot_sem.at[k]) for k, (p, q) in enumerate(zip(tots_i, tots))]
    pairs = [(p, q, n * 2 + k, pl.ds(16 * k, 16)) for k in range(2) for n, (p, q) in enumerate(((decoded_i, decoded), (images_grad_i, images_grad)))]
    ins = [pltpu.make_async_copy(p.at[rows], hold.at[k], sem.at[k]) for p, q, k, rows in pairs]
    backs = [pltpu.make_async_copy(hold.at[k], q.at[rows], sem.at[4 + k]) for p, q, k, rows in pairs]
    for cp in small + ins:
        cp.start()
    loss[0] = loss_i[0]
    wait_all(small)
    spots, _ = places(dp)

    def piece(name):
        g, at, n = spots[name]
        return tots[g][:, at:at + n]
    for k, name in enumerate(("ef", "es", "et", None, "df", "ds", "dt")):
        if name:
            outs[k][...] = piece(name)
    outs[3][...] = piece("eo")[0:64 // dp]
    for k in range(4):
        outs[7][16 * k:16 * k + 16] = piece(k)
    for ref, v in zip(outs[8:], bias_rows(piece("bias"), 64 // dp)):
        ref[...] = v
    last = [pltpu.make_async_copy(p, q, out_sem.at[k]) for k, (p, q) in enumerate(zip(outs, outs_h))]
    for p, q in zip(ins, backs):
        p.wait()
        q.start()
    for cp in last:
        cp.start()
    wait_all(last + backs)


U = dict(B=4, nC=32, C=1, K=1, nQ=16, Q=1, nF=16, F=1, nJ=32, J=1, nG=16, Qr=1, nN=32)


def per_device(images, targets, pixel_mask, ef, es, et, eo, eba, ebb, ebc, ebd, df, ds, dt, do, dba, dbb, dbc, dbd):
    dp = lax.axis_size("dp")
    nz = dp // 2
    widths = places(dp)[1]
    chips = len(chip_steps(nz))
    vm = pl.BlockSpec(memory_space=pltpu.VMEM)
    far = pl.BlockSpec(memory_space=pl.ANY)
    smem = pl.BlockSpec(memory_space=pltpu.SMEM)
    sem = pltpu.SemaphoreType.DMA
    V = lambda shape, dt: pltpu.VMEM(shape, dt)
    S = jax.ShapeDtypeStruct
    args = [images[0], targets[0], pixel_mask[0], ef.T, es.T, et.T, eo, df.T, ds.T, dt.T, do.T]
    args += [b.reshape(1, -1) for b in (eba, ebb, ebc, ebd, dba, dbb, dbc, dbd)]
    sums = []
    for w in widths:
        sums += [V((nz, 2, 2, 16, w), BF16)] * 2 + [V((chips, 16, w), BF16)]
    big = S((32, 128, 256), BF16)
    tots = [S((16, w), F32) for w in widths]
    decoded, images_grad, loss, *kept = pl.pallas_call(
        functools.partial(main_kernel, U),
        out_shape=[big, big, S((1,), F32), *tots],
        in_specs=[far] * 19, out_specs=[far, far, smem, vm, vm, vm],
        scratch_shapes=[V(a.shape, a.dtype) for a in args] + [
            V((32, 64, 512), BF16), V((34, 64, 512), BF16), V((32, 64, 512), F32),
            V((34, 64, 256), BF16), V((34, 64, 256), BF16), V((32, 64, 128), BF16),
            V((34, 64, 256), BF16), V((34, 64, 256), BF16), V((34, 64, 256), BF16)] + [V((32, 64, 128), F32)] * 6 + [
            V((32, 64, 512), F32), V((32, 64, 512), F32), V((32, 64, 512), BF16),
            V((34, 64, 512), BF16), V((32, 64, 512), BF16), V((34, 64, 256), BF16), V((34, 64, 256), BF16),
            V((4, 2, 128, 128), F32),
            V((3, 256, 512), BF16)] + [V((4, 256, 256), BF16)] * 8 + [
            V((3, 512, 256), BF16), V((128, 512), BF16), V((128, 512), BF16),
            V((8, 1, 512), F32), V((8, 8, 512), F32), V((8, 128), F32), V((32, 64, 512), BF16)]
        + [V((nz, 2, 2, 2, 16, w), BF16) for w in widths] * 2 + sums
        + [sem((16,)), sem((4,)), sem((6,))] + [sem((chips + nz,))] * 2 + [sem((nz + 4,))] * 2 + [sem((chips + nz,))] * 2 + [sem((chips + 3,))] * 6,
        compiler_params=pltpu.CompilerParams(collective_id=0, has_side_effects=True, vmem_limit_bytes=63 * 2**20),
    )(*args)
    f = lambda *s: S(s, F32)
    grads = [f(16, 2304 // dp), f(16, 576 // dp), f(16, 576 // dp), f(64 // dp, 64), f(16, 256 // dp),
             f(16, 576 // dp), f(16, 576 // dp), f(64, 576 // dp)] + [f(1, s // dp) for s in (64, 64, 64, 256) * 2]
    outs = pl.pallas_call(
        last_kernel,
        out_shape=[big, big, S((1,), F32)] + grads,
        in_specs=[far, far, smem, far, far, far], out_specs=[far, far, smem] + [far] * 16,
        scratch_shapes=[V(g.shape, F32) for g in grads + tots] + [V((4, 16, 128, 256), BF16), sem((8,)), sem((3,)), sem((16,))],
        compiler_params=pltpu.CompilerParams(vmem_limit_bytes=60 * 2**20),
    )(decoded, images_grad, loss, *kept)
    decoded, images_grad, loss, g_ef, g_es, g_et, g_eo, g_df, g_ds, g_dt, g_do = outs[:11]
    bs = [b.reshape(-1) for b in outs[11:]]
    return (decoded[None], images_grad[None], loss, g_ef.T, g_es.T, g_et.T, g_eo, *bs[:4],
            g_df.T, g_ds.T, g_dt.T, g_do.T, *bs[4:])


def solution(mesh):
    img, w, b = P(("dp", "fsdp"), None, None, None), P("dp", "fsdp"), P("dp")
    placed = (img, img, P(("dp", "fsdp"), None, None)) + (w,) * 4 + (b,) * 4 + (w,) * 4 + (b,) * 4
    return jax.shard_map(
        per_device, mesh=mesh, in_specs=placed,
        out_specs=(img, img, P(("dp", "fsdp"))) + (w,) * 4 + (b,) * 4 + (w,) * 4 + (b,) * 4,
        check_vma=False)
```
